128 devices in a mesh: blk: 16 (over z, y), grid: 8 (over x, core).
Axes of the slice: x: 4, y: 4, z: 4, core: 2. Of those that a mesh axis runs over, the one named last changes fastest.
Arguments:
- queries: bfloat16 [81920, 32, 128], P(('blk', 'grid')), may hold values from -100 to 100
- keys: bfloat16 [81920, 8, 128], P(('blk', 'grid')), may hold values from -5 to 5
- values: bfloat16 [81920, 8, 128], P(('blk', 'grid')), may hold values from -40 to 40
- vert_blocks: int32 [8, 12], replicated, may hold values from 0 to 1279, as said below
- slash_offsets: int32 [8, 4], replicated, may hold values from 0 to 7, as said below
- far_blocks: int32 [8, 1280], replicated, may hold values from -1 to 1271, as said below
Outputs:
- attended: bfloat16 [81920, 32, 128], P(('blk', 'grid'))
The draws below stay inside these ranges and needn't reach their ends.
Inputs may be any that keep to these rules, and one draw needn't show every extreme that they name: `vert_blocks`: each key head has 12 different vertical blocks. Over all heads together at most 1 vertical blocks lie among the 10 blocks of one device, and exactly 1 among those of some device. `slash_offsets`: each key head's list holds 4 different offsets, 0 among them; the list of some head holds 7. An entry far_blocks[h, b] is -1 or a block at most b - 8 that is not a vertical block of head h. The entries of all heads for the 10 query blocks of one device name at most 2 blocks among the 10 blocks of any one device, and exactly 2 for some pair of devices.
All inputs are finite; a program needn't handle non-finite values.
Results may differ from the reference program's by a relative error of at most 0.0046.
Values may be sent and summed in bfloat16 or wider, within the bound.
No kernel may reach another device: no remote copies, remote signals or barrier semaphores. Data moves between devices by JAX's collectives and lax.ppermute only.
A program may use at most 448 MiB of HBM per device.

```python
import jax
import jax.numpy as jnp
from jax import lax

HQ = 32
HK = 8
DH = 128
BS = 64
NW = 8
NSL = 4
NV = 12
G = 4
BPD = 10
TOKENS = 81920
NB = 1280
CAP = 2
CAPV = 1
DEVICES = 128


def key_base(key):
    return jnp.clip(jax.random.normal(key, (TOKENS, HK, DH), jnp.float32), -5.0, 5.0)


def vertical_layout(key):
    key = jax.random.fold_in(key, 3)
    order_key, base_key = jax.random.split(key)
    slot_order = jax.random.permutation(order_key, DEVICES * CAPV)[:HK * NV]
    owner_dev = slot_order // CAPV
    base_block = jax.random.randint(base_key, (DEVICES,), 0, BPD)
    local_block = (base_block[owner_dev] + slot_order % CAPV) % BPD
    return (owner_dev * BPD + local_block).reshape(HK, NV).astype(jnp.int32)


def far_layout(key):
    verticals = vertical_layout(key)
    key = jax.random.fold_in(key, 9)
    order_key, slot_key, local_key = jax.random.split(key, 3)
    req_total = HK * BPD
    slot_total = DEVICES * CAP
    request_scores = jax.random.randint(order_key, (DEVICES, req_total), 0, 4096) * req_total + jnp.arange(req_total)[None, :]
    request_order = jnp.argsort(request_scores, axis=1)
    request_place = jnp.argsort(request_order, axis=1)
    source = jnp.arange(DEVICES)[:, None]
    slot_owner = jnp.arange(slot_total)[None, :] // CAP
    allowed = (slot_owner >= 1) & (slot_owner < source)
    slot_scores = jax.random.randint(slot_key, (DEVICES, slot_total), 0, 4096) * slot_total + jnp.arange(slot_total)[None, :]
    slot_scores = jnp.where(allowed, slot_scores, 4096 * slot_total + jnp.arange(slot_total)[None, :])
    slot_order = jnp.argsort(slot_scores, axis=1)
    later_place = jnp.clip(request_place - CAP, 0, slot_total - 1)
    later_owner = jnp.take_along_axis(slot_order, later_place, axis=1) // CAP
    available = CAP * jnp.maximum(source - 1, 0)
    owner_dev = jnp.where(request_place < CAP, 0, later_owner)
    present = (source >= 1) & ((request_place < CAP) | (request_place - CAP < available))
    local_block = jax.random.randint(local_key, (DEVICES, req_total), 0, BPD - NW + 1)
    far_block = owner_dev * BPD + local_block
    request_head = jnp.arange(req_total) // BPD
    head_verticals = verticals[request_head]
    clash_found = jnp.any(head_verticals[None, :, :] == far_block[:, :, None], axis=2)
    result = jnp.where(present & jnp.logical_not(clash_found), far_block, -1)
    return result.reshape(DEVICES, HK, BPD).transpose(1, 0, 2).reshape(HK, NB).astype(jnp.int32)


def draw_keys(key, part):
    return key_base(key).astype(jnp.bfloat16)


def draw_queries(key, part):
    key = jax.random.fold_in(key, 7)
    fresh_draw = jnp.clip(jax.random.normal(key, (TOKENS, HQ, DH), jnp.float32), -5.0, 5.0)
    return fresh_draw.astype(jnp.bfloat16)


def draw_vert_blocks(key, part):
    return vertical_layout(key)


def draw_slash_offsets(key, part):
    key = jax.random.fold_in(key, 4)
    order_key, star_key, place_key = jax.random.split(key, 3)
    span_len = NW - 1
    order_scores = jax.random.randint(order_key, (HK, span_len), 0, 4096) * span_len + jnp.arange(span_len)[None, :]
    shuffled = jnp.argsort(order_scores, axis=1) + 1
    star_head = jax.random.randint(star_key, (), 0, HK)
    last_place = jnp.argmax(shuffled == span_len, axis=1)
    columns = jnp.arange(span_len)[None, :]
    swapped = jnp.where(columns == 0, span_len, jnp.where(columns == last_place[:, None], shuffled[:, :1], shuffled))
    shuffled = jnp.where((jnp.arange(HK) == star_head)[:, None], swapped, shuffled)
    chosen = jnp.concatenate([jnp.zeros((HK, 1), jnp.int32), shuffled[:, :NSL - 1].astype(jnp.int32)], axis=1)
    place_scores = jax.random.randint(place_key, (HK, NSL), 0, 4096) * NSL + jnp.arange(NSL)[None, :]
    return jnp.take_along_axis(chosen, jnp.argsort(place_scores, axis=1), axis=1).astype(jnp.int32)


def draw_far_blocks(key, part):
    return far_layout(key)


def shard_levels(rng, dims, cuts, low, largest):
    loudness = 1.0
    for dim, parts in cuts:
        heights = jax.random.uniform(jax.random.fold_in(jax.random.fold_in(rng, 6), dim), (parts,), jnp.float32, low / len(cuts), largest / len(cuts))
        loudness = loudness * jnp.repeat(jnp.exp(heights), dims[dim] // parts).reshape((-1,) + (1,) * (len(dims) - 1 - dim))
    return loudness


def scatter_about(rng, dims, scale, most, shards=(), kind=jnp.bfloat16):
    loudness = shard_levels(rng, dims, shards, -0.22, 0.18) if shards else 1.0
    entries = jax.random.normal(rng, dims, jnp.float32) * scale * loudness
    return jnp.minimum(jnp.maximum(entries, -most), most).astype(kind)


def setup_inputs(seed: int = 0) -> dict:
    seeds = jax.random.split(jax.random.key(seed), 7)
    queries = draw_queries(jax.random.fold_in(seeds[6], 71), 0)
    keys = draw_keys(jax.random.fold_in(seeds[6], 71), 0)
    values = scatter_about(seeds[2], (TOKENS, HK, DH), 8.0, 40.0, ((0, 128),))
    vert_blocks = draw_vert_blocks(jax.random.fold_in(seeds[6], 71), 0)
    slash_offsets = draw_slash_offsets(jax.random.fold_in(seeds[6], 71), 0)
    far_blocks = draw_far_blocks(jax.random.fold_in(seeds[6], 71), 0)
    return dict(queries=queries, keys=keys, values=values, vert_blocks=vert_blocks, slash_offsets=slash_offsets, far_blocks=far_blocks)


def far_partial(q_tile, k_tile, v_tile, score_scale):
    scores = jnp.einsum("...tgd,...kd->...tgk", q_tile.astype(jnp.float32), k_tile.astype(jnp.float32)) * score_scale
    top_score = jnp.max(scores, axis=-1)
    weights = jnp.exp(scores - top_score[..., None])
    weight_sum = jnp.sum(weights, axis=-1)
    low_weights = lax.optimization_barrier(weights.astype(jnp.bfloat16)).astype(jnp.float32)
    mixed_sum = jnp.einsum("...tgk,...kd->...tgd", low_weights, v_tile.astype(jnp.float32))
    partial_out = (mixed_sum / weight_sum[..., None]).astype(jnp.bfloat16)
    return partial_out, top_score + jnp.log(weight_sum)


def reference(queries, keys, values, vert_blocks, slash_offsets, far_blocks):
    score_scale = DH ** -0.5
    block_total = queries.shape[0] // BS
    q_blocks = queries.reshape(block_total, BS, HK, G, DH)
    k_blocks = keys.reshape(block_total, BS, HK, DH)
    v_blocks = values.reshape(block_total, BS, HK, DH)
    front_pad = jnp.zeros((NW - 1, BS, HK, DH), keys.dtype)
    k_padded = jnp.concatenate([front_pad, k_blocks], axis=0)
    v_padded = jnp.concatenate([front_pad, v_blocks], axis=0)
    causal_ok = jnp.arange(BS)[None, :] <= jnp.arange(BS)[:, None]
    group_count = block_total // BPD
    results = []
    for kv_head in range(HK):
        offsets = slash_offsets[kv_head]
        verticals = vert_blocks[kv_head]
        far_row = far_blocks[kv_head]
        q_head = q_blocks[:, :, kv_head]
        k_head = k_padded[:, :, kv_head]
        v_head = v_padded[:, :, kv_head]
        vert_keys = k_blocks[verticals, :, kv_head].astype(jnp.float32)
        vert_vals = v_blocks[verticals, :, kv_head].astype(jnp.float32)
        far_keys_all = k_blocks[:, :, kv_head]
        far_vals_all = v_blocks[:, :, kv_head]

        def one_group(group_index):
            first_block = group_index * BPD
            query_block = first_block + jnp.arange(BPD, dtype=jnp.int32)
            q_here = lax.dynamic_slice_in_dim(q_head, first_block, BPD, 0).astype(jnp.float32)
            near_index = query_block[:, None] + (NW - 1) - offsets[None, :]
            near_keys = k_head[near_index].astype(jnp.float32)
            near_vals = v_head[near_index].astype(jnp.float32)
            near_scores = jnp.einsum("btgd,bikd->btgik", q_here, near_keys) * score_scale
            vert_scores = jnp.einsum("btgd,ikd->btgik", q_here, vert_keys) * score_scale
            near_ok = (query_block[:, None] - offsets[None, :]) >= 0
            near_mask = near_ok[:, None, None, :, None] & ((offsets != 0)[None, None, None, :, None] | causal_ok[None, :, None, None, :])
            vert_ok = (verticals[None, :] <= query_block[:, None] - NW)[:, None, None, :, None]
            scores = jnp.concatenate([jnp.where(near_mask, near_scores, -jnp.inf), jnp.where(vert_ok, vert_scores, -jnp.inf)], axis=3)
            top_score = jnp.max(scores, axis=(3, 4))
            weights = jnp.exp(scores - top_score[..., None, None])
            weight_sum = jnp.sum(weights, axis=(3, 4))
            low_weights = lax.optimization_barrier(weights.astype(jnp.bfloat16)).astype(jnp.float32)
            mixed_sum = jnp.einsum("btgik,bikd->btgd", low_weights[:, :, :, :NSL], near_vals)
            mixed_sum = mixed_sum + jnp.einsum("btgik,ikd->btgd", low_weights[:, :, :, NSL:], vert_vals)
            local_out = mixed_sum / weight_sum[..., None]
            local_lse = top_score + jnp.log(weight_sum)
            far_index = lax.dynamic_slice_in_dim(far_row, first_block, BPD, 0)
            far_ok = (far_index >= 0)[:, None, None]
            safe_index = jnp.maximum(far_index, 0)
            far_out, far_lse = far_partial(q_here, far_keys_all[safe_index], far_vals_all[safe_index], score_scale)
            joint_max = jnp.maximum(local_lse, jnp.where(far_ok, far_lse, local_lse))
            local_weight = jnp.exp(local_lse - joint_max)
            far_weight = jnp.where(far_ok, jnp.exp(far_lse - joint_max), 0.0)
            far_part = jnp.where(far_ok[..., None], far_out.astype(jnp.float32), 0.0)
            merged = (local_weight[..., None] * local_out + far_weight[..., None] * far_part) / (local_weight + far_weight)[..., None]
            return merged.astype(jnp.bfloat16)

        per_head = lax.map(one_group, jnp.arange(group_count, dtype=jnp.int32))
        results.append(per_head.reshape(block_total, BS, G, DH))
    return jnp.stack(results, axis=2).reshape(queries.shape)
```

```python
import functools

import jax
import jax.numpy as jnp
from jax import lax
from jax.experimental import pallas as pl
from jax.experimental.pallas import tpu as pltpu
from jax.sharding import PartitionSpec as P

BS = 64
NW = 8
CAP = 2
AXES = ("blk", "grid")
MASKED = -1e30
LOG2E = 1.4426950408889634


def local_kernel(
    core_sm, slot_sm, off_sm, first_sm,
    q_ref, ko_ref, vo_ref, kh_ref, vh_ref, bias_ref, mine_hbm, other_hbm,
    out_ref, lse_ref,
    kx, vx, kv_buf, vv_buf, sems,
    *, heads, verts, blocks, group, near, scale,
):
    h = pl.program_id(0)
    halo = kh_ref.shape[1]
    own = ko_ref.shape[1]

    def fetch(head, buf):
        def from_pair(k_src, v_src):
            for i in range(verts):
                slot = slot_sm[head, i]
                rows = pl.ds(i * BS, BS)
                pltpu.make_async_copy(k_src.at[slot], kv_buf.at[buf, rows], sems.at[buf, 0]).start()
                pltpu.make_async_copy(v_src.at[slot], vv_buf.at[buf, rows], sems.at[buf, 1]).start()

        @pl.when(core_sm[0] == 0)
        def _():
            from_pair(mine_hbm, other_hbm)

        @pl.when(core_sm[0] != 0)
        def _():
            from_pair(other_hbm, mine_hbm)

    @pl.when(h == 0)
    def _():
        fetch(0, 0)

    @pl.when(h + 1 < heads)
    def _():
        fetch(h + 1, (h + 1) % 2)

    kx[0:halo] = kh_ref[0]
    kx[halo : halo + own] = ko_ref[0]
    vx[0:halo] = vh_ref[0]
    vx[halo : halo + own] = vo_ref[0]
    cur = h % 2
    pltpu.make_async_copy(kv_buf.at[cur], kv_buf.at[cur], sems.at[cur, 0]).wait()
    pltpu.make_async_copy(vv_buf.at[cur], vv_buf.at[cur], sems.at[cur, 1]).wait()

    t_pos = lax.broadcasted_iota(jnp.int32, (BS, near * BS), 0)
    u_pos = lax.broadcasted_iota(jnp.int32, (BS, near * BS), 1)
    causal_bias = jnp.where((u_pos < BS) & (u_pos > t_pos), MASKED, 0.0)
    lane = lax.broadcasted_iota(jnp.int32, (1, near * BS), 1) // BS

    def one_block(b, carry):
        rows = pl.multiple_of(b * BS, BS)
        q = q_ref[0, :, pl.ds(rows, BS), :].reshape(group * BS, q_ref.shape[3])
        k_parts = []
        v_parts = []
        row_bias = jnp.zeros((1, near * BS), jnp.float32)
        for i in range(near):
            off = off_sm[h, i]
            start = pl.multiple_of((b + NW - 1 - off) * BS, BS)
            k_parts.append(kx[pl.ds(start, BS), :])
            v_parts.append(vx[pl.ds(start, BS), :])
            miss = jnp.where(first_sm[0] + b < off, MASKED, 0.0)
            row_bias = jnp.where(lane == i, miss, row_bias)
        k_near = jnp.concatenate(k_parts, axis=0)
        v_near = jnp.concatenate(v_parts, axis=0)
        dims = (((1,), (1,)), ((), ()))
        s_near = lax.dot_general(q, k_near, dims, preferred_element_type=jnp.float32)
        near_bias = causal_bias + row_bias
        s_near = (s_near.reshape(group, BS, near * BS) + near_bias[None]).reshape(s_near.shape)
        s_vert = lax.dot_general(q, kv_buf[cur], dims, preferred_element_type=jnp.float32)
        s_vert = s_vert + bias_ref[0, pl.ds(b, 1), :]
        top = jnp.maximum(
            jnp.max(s_near, axis=1, keepdims=True), jnp.max(s_vert, axis=1, keepdims=True)
        )
        p_near = jnp.exp2((s_near - top) * (scale * LOG2E))
        p_vert = jnp.exp2((s_vert - top) * (scale * LOG2E))
        total = jnp.sum(p_near, axis=1, keepdims=True) + jnp.sum(p_vert, axis=1, keepdims=True)
        acc = jnp.dot(p_near.astype(jnp.bfloat16), v_near, preferred_element_type=jnp.float32)
        acc = acc + jnp.dot(
            p_vert.astype(jnp.bfloat16), vv_buf[cur], preferred_element_type=jnp.float32
        )
        out_ref[0, b] = acc / total
        lse = top * scale + jnp.log(total)
        wide = jnp.broadcast_to(lse, (lse.shape[0], 128))
        lse_ref[0, b] = wide.T[0:1, :]
        return carry

    lax.fori_loop(0, blocks, one_block, 0)


def merge_kernel(
    slot_sm, valid_sm,
    q_ref, local_ref, lse_ref, far_hbm,
    out_ref,
    kv_buf, wide_out, sems,
    *, heads, blocks, group, scale,
):
    b = pl.program_id(0)

    def fetch(block, buf):
        for h in range(heads):
            slot = slot_sm[h * blocks + block]
            pltpu.make_async_copy(far_hbm.at[slot], kv_buf.at[buf, h], sems.at[buf]).start()

    @pl.when(b == 0)
    def _():
        fetch(0, 0)

    @pl.when(b + 1 < blocks)
    def _():
        fetch(b + 1, (b + 1) % 2)

    cur = b % 2
    pltpu.make_async_copy(kv_buf.at[cur], kv_buf.at[cur], sems.at[cur]).wait()
    rows = group * BS
    for h in range(heads):
        q = q_ref[h].reshape(rows, q_ref.shape[3])
        s = lax.dot_general(
            q, kv_buf[cur, h, 0], (((1,), (1,)), ((), ())), preferred_element_type=jnp.float32
        )
        top = jnp.max(s, axis=1, keepdims=True)
        p = jnp.exp2((s - top) * (scale * LOG2E))
        total = jnp.sum(p, axis=1, keepdims=True)
        acc = jnp.dot(
            p.astype(jnp.bfloat16), kv_buf[cur, h, 1], preferred_element_type=jnp.float32
        )
        far_out = (acc / total).astype(jnp.bfloat16).astype(jnp.float32)
        far_lse = top * scale + jnp.log(total)
        local_out = local_ref[h, 0]
        local_lse = jnp.broadcast_to(lse_ref[h, 0], (128, rows)).T
        joint = jnp.maximum(local_lse, far_lse)
        a = jnp.exp(local_lse - joint)
        c = jnp.exp(far_lse - joint)
        merged = (a * local_out + c * far_out) / (a + c)
        ok = valid_sm[h * blocks + b] > 0
        merged = jnp.where(ok, merged, local_out)
        for g in range(group):
            wide_out[pl.ds(h * group + g, BS, stride=heads * group), :] = merged[
                g * BS : (g + 1) * BS
            ]
    out_ref[...] = wide_out[...].reshape(out_ref.shape).astype(jnp.bfloat16)


def shards(queries, keys, values, vert_blocks, slash_offsets, far_blocks):
    tok, q_heads, dh = queries.shape
    heads = keys.shape[1]
    group = q_heads // heads
    blocks = tok // BS
    verts = vert_blocks.shape[1]
    near = slash_offsets.shape[1]
    reqs = heads * blocks
    devices = lax.axis_size(AXES)
    rank = lax.axis_index(AXES)
    core = rank % 2
    scale = dh**-0.5
    halo_rows = (NW - 1) * BS
    rows = group * BS

    vert_flat = vert_blocks.reshape(-1)
    is_mine = vert_flat // blocks == rank
    pick = jnp.max(jnp.where(is_mine, jnp.arange(heads * verts), 0))
    pick_head = pick // verts
    pick_row = jnp.clip(jnp.max(jnp.where(is_mine, vert_flat - rank * blocks, 0)), 0, blocks - 1) * BS
    v_key = lax.dynamic_slice(keys, (pick_row, pick_head, 0), (BS, 1, dh)).reshape(1, 1, BS, dh)
    v_val = lax.dynamic_slice(values, (pick_row, pick_head, 0), (BS, 1, dh)).reshape(1, 1, BS, dh)
    vert_send = jnp.broadcast_to(
        jnp.concatenate([v_key, v_val], axis=1), (devices // 2, 2, BS, dh)
    ).reshape(devices, BS, dh)
    vert_mine = lax.all_to_all(vert_send, AXES, split_axis=0, concat_axis=0, tiled=True)

    k_t = keys.transpose(1, 0, 2)
    v_t = values.transpose(1, 0, 2)
    rim = jnp.stack([k_t[:, tok - halo_rows :], v_t[:, tok - halo_rows :]])
    before = lax.ppermute(rim, AXES, [(i, i + 1) for i in range(devices - 1)])

    all_far = far_blocks.reshape(heads, devices, blocks).transpose(1, 0, 2).reshape(devices, reqs)
    earlier = (jnp.arange(reqs)[:, None] < jnp.arange(reqs)[None, :]).astype(jnp.float32)
    asked = (all_far >= 0) & (all_far // blocks == rank)
    place = jnp.dot(asked.astype(jnp.float32), earlier).astype(jnp.int32)
    tile = (jnp.arange(reqs)[None, :] // blocks) * blocks + all_far - rank * blocks
    wanted = asked[:, None, :] & (place[:, None, :] == jnp.arange(CAP)[None, :, None])
    send_tile = jnp.max(jnp.where(wanted, tile[:, None, :], 0), axis=2).reshape(-1)
    tiles = jnp.stack(
        [k_t.reshape(heads * blocks, BS, dh), v_t.reshape(heads * blocks, BS, dh)], axis=1
    )
    far_send = tiles[send_tile]
    far_send, vert_mine = lax.optimization_barrier((far_send, vert_mine))
    vert_other = lax.ppermute(vert_mine, AXES, [(i, i ^ 1) for i in range(devices)])
    far_got = lax.all_to_all(far_send, AXES, split_axis=0, concat_axis=0, tiled=True)

    my_far = lax.dynamic_slice_in_dim(far_blocks, rank * blocks, blocks, 1).reshape(-1)
    valid = (my_far >= 0).astype(jnp.int32)
    owner = jnp.where(my_far >= 0, my_far // blocks, -1)
    same = owner[:, None] == owner[None, :]
    my_place = jnp.sum(same & (jnp.arange(reqs)[None, :] < jnp.arange(reqs)[:, None]), axis=1)
    got_slot = jnp.where(my_far >= 0, owner * CAP + jnp.minimum(my_place, CAP - 1), 0)

    q_t = queries.reshape(tok, heads, group, dh).transpose(1, 2, 0, 3)
    zero_at = jnp.argmax((slash_offsets == 0).astype(jnp.int32), axis=1)
    order = (zero_at[:, None] + jnp.arange(near)[None, :]) % near
    offsets = jnp.sum(
        jnp.where(order[:, :, None] == jnp.arange(near)[None, None, :], slash_offsets[:, None, :], 0),
        axis=2,
    )
    my_blocks = rank * blocks + jnp.arange(blocks)
    vert_ok = vert_blocks[:, None, :] <= my_blocks[None, :, None] - NW
    vert_bias = jnp.repeat(jnp.where(vert_ok, 0.0, MASKED).astype(jnp.float32), BS, axis=2)

    by_head = lambda *tail: pl.BlockSpec((1,) + tail, lambda h, *_: (h,) + (0,) * len(tail))
    local_out, local_lse = pl.pallas_call(
        functools.partial(
            local_kernel, heads=heads, verts=verts, blocks=blocks, group=group, near=near,
            scale=scale,
        ),
        grid_spec=pltpu.PrefetchScalarGridSpec(
            num_scalar_prefetch=4,
            grid=(heads,),
            in_specs=[
                by_head(group, tok, dh),
                by_head(tok, dh),
                by_head(tok, dh),
                by_head(halo_rows, dh),
                by_head(halo_rows, dh),
                by_head(blocks, verts * BS),
                pl.BlockSpec(memory_space=pl.ANY),
                pl.BlockSpec(memory_space=pl.ANY),
            ],
            out_specs=[by_head(blocks, rows, dh), by_head(blocks, 1, rows)],
            scratch_shapes=[
                pltpu.VMEM((halo_rows + tok, dh), jnp.bfloat16),
                pltpu.VMEM((halo_rows + tok, dh), jnp.bfloat16),
                pltpu.VMEM((2, verts * BS, dh), jnp.bfloat16),
                pltpu.VMEM((2, verts * BS, dh), jnp.bfloat16),
                pltpu.SemaphoreType.DMA((2, 2)),
            ],
        ),
        out_shape=[
            jax.ShapeDtypeStruct((heads, blocks, rows, dh), jnp.float32),
            jax.ShapeDtypeStruct((heads, blocks, 1, rows), jnp.float32),
        ],
        compiler_params=pltpu.CompilerParams(vmem_limit_bytes=40 * 1024 * 1024),
        cost_estimate=pl.CostEstimate(
            flops=4 * heads * blocks * rows * dh * (near + verts) * BS,
            bytes_accessed=40_000_000,
            transcendentals=heads * blocks * rows * (near + verts) * BS,
        ),
        name="local_attention",
    )(
        core.reshape(1).astype(jnp.int32),
        (vert_blocks // blocks).astype(jnp.int32),
        offsets.astype(jnp.int32),
        (rank * blocks).reshape(1).astype(jnp.int32),
        q_t, k_t, v_t, before[0], before[1], vert_bias, vert_mine, vert_other,
    )

    attended = pl.pallas_call(
        functools.partial(merge_kernel, heads=heads, blocks=blocks, group=group, scale=scale),
        grid_spec=pltpu.PrefetchScalarGridSpec(
            num_scalar_prefetch=2,
            grid=(blocks,),
            in_specs=[
                pl.BlockSpec((heads, group, BS, dh), lambda b, *_: (0, 0, b, 0)),
                pl.BlockSpec((heads, 1, rows, dh), lambda b, *_: (0, b, 0, 0)),
                pl.BlockSpec((heads, 1, 1, rows), lambda b, *_: (0, b, 0, 0)),
                pl.BlockSpec(memory_space=pl.ANY),
            ],
            out_specs=pl.BlockSpec((BS, q_heads, dh), lambda b, *_: (b, 0, 0)),
            scratch_shapes=[
                pltpu.VMEM((2, heads, 2, BS, dh), jnp.bfloat16),
                pltpu.VMEM((BS * q_heads, dh), jnp.float32),
                pltpu.SemaphoreType.DMA((2,)),
            ],
        ),
        out_shape=jax.ShapeDtypeStruct((tok, q_heads, dh), jnp.bfloat16),
        compiler_params=pltpu.CompilerParams(vmem_limit_bytes=40 * 1024 * 1024),
        cost_estimate=pl.CostEstimate(
            flops=4 * heads * blocks * rows * dh * BS,
            bytes_accessed=25_000_000,
            transcendentals=heads * blocks * rows * BS,
        ),
        name="far_merge",
    )(got_slot.astype(jnp.int32), valid, q_t, local_out, local_lse, far_got)
    return attended


def solution(mesh):
    split = P(AXES, None, None)
    return jax.shard_map(
        shards,
        mesh=mesh,
        in_specs=(split, split, split, P(), P(), P()),
        out_specs=split,
        check_vma=False,
    )
```

```python
import functools

import jax
import jax.numpy as jnp
from jax import lax
from jax.experimental import pallas as pl
from jax.experimental.pallas import tpu as pltpu
from jax.sharding import PartitionSpec as P

BS = 64
NW = 8
CAP = 2
AXES = ("blk", "grid")
MASKED = -1e30
LOG2E = 1.4426950408889634


def local_kernel(
    core_sm, slot_sm, off_sm, first_sm,
    q_ref, ko_ref, vo_ref, kh_ref, vh_ref, bias_ref, mine_hbm, other_hbm,
    out_ref, lse_ref,
    kx, vx, kv_buf, vv_buf, sems,
    *, heads, verts, blocks, group, near, scale,
):
    h = pl.program_id(0)
    halo = kh_ref.shape[1]
    own = ko_ref.shape[1]

    def fetch(head, buf):
        def from_pair(k_src, v_src):
            for i in range(verts):
                slot = slot_sm[head, i]
                rows = pl.ds(i * BS, BS)
                pltpu.make_async_copy(k_src.at[slot], kv_buf.at[buf, rows], sems.at[buf, 0]).start()
                pltpu.make_async_copy(v_src.at[slot], vv_buf.at[buf, rows], sems.at[buf, 1]).start()

        @pl.when(core_sm[0] == 0)
        def _():
            from_pair(mine_hbm, other_hbm)

        @pl.when(core_sm[0] != 0)
        def _():
            from_pair(other_hbm, mine_hbm)

    @pl.when(h == 0)
    def _():
        fetch(0, 0)

    @pl.when(h + 1 < heads)
    def _():
        fetch(h + 1, (h + 1) % 2)

    kx[0:halo] = kh_ref[0]
    kx[halo : halo + own] = ko_ref[0]
    vx[0:halo] = vh_ref[0]
    vx[halo : halo + own] = vo_ref[0]
    cur = h % 2
    pltpu.make_async_copy(kv_buf.at[cur], kv_buf.at[cur], sems.at[cur, 0]).wait()
    pltpu.make_async_copy(vv_buf.at[cur], vv_buf.at[cur], sems.at[cur, 1]).wait()

    t_pos = lax.broadcasted_iota(jnp.int32, (group * BS, near * BS), 0) // group
    u_pos = lax.broadcasted_iota(jnp.int32, (group * BS, near * BS), 1)
    causal_bias = jnp.where((u_pos < BS) & (u_pos > t_pos), MASKED, 0.0)
    lane = lax.broadcasted_iota(jnp.int32, (1, near * BS), 1) // BS

    def one_block(b, carry):
        rows = pl.multiple_of(b * group * BS, group * BS)
        q = q_ref[0, pl.ds(rows, group * BS), :]
        k_parts = []
        v_parts = []
        row_bias = jnp.zeros((1, near * BS), jnp.float32)
        for i in range(near):
            off = off_sm[h, i]
            start = pl.multiple_of((b + NW - 1 - off) * BS, BS)
            k_parts.append(kx[pl.ds(start, BS), :])
            v_parts.append(vx[pl.ds(start, BS), :])
            miss = jnp.where(first_sm[0] + b < off, MASKED, 0.0)
            row_bias = jnp.where(lane == i, miss, row_bias)
        k_near = jnp.concatenate(k_parts, axis=0)
        v_near = jnp.concatenate(v_parts, axis=0)
        dims = (((1,), (1,)), ((), ()))
        s_near = lax.dot_general(q, k_near, dims, preferred_element_type=jnp.float32)
        s_near = s_near + (causal_bias + row_bias)
        s_vert = lax.dot_general(q, kv_buf[cur], dims, preferred_element_type=jnp.float32)
        s_vert = s_vert + bias_ref[0, pl.ds(b, 1), :]
        top = jnp.maximum(
            jnp.max(s_near, axis=1, keepdims=True), jnp.max(s_vert, axis=1, keepdims=True)
        )
        p_near = jnp.exp2((s_near - top) * (scale * LOG2E))
        p_vert = jnp.exp2((s_vert - top) * (scale * LOG2E))
        total = jnp.sum(p_near, axis=1, keepdims=True) + jnp.sum(p_vert, axis=1, keepdims=True)
        acc = jnp.dot(p_near.astype(jnp.bfloat16), v_near, preferred_element_type=jnp.float32)
        acc = acc + jnp.dot(
            p_vert.astype(jnp.bfloat16), vv_buf[cur], preferred_element_type=jnp.float32
        )
        out_ref[0, b] = acc / total
        lse = top * scale + jnp.log(total)
        lse_ref[0, pl.ds(b, 1), :] = jnp.broadcast_to(lse, (lse.shape[0], 128)).T[0:1, :]
        return carry

    lax.fori_loop(0, blocks, one_block, 0)


def merge_kernel(
    slot_sm, valid_sm,
    q_ref, local_ref, lse_ref, far_hbm,
    out_ref,
    kv_buf, sems,
    *, heads, blocks, group, scale,
):
    b = pl.program_id(0)

    def fetch(block, buf):
        for h in range(heads):
            slot = slot_sm[h * blocks + block]
            pltpu.make_async_copy(far_hbm.at[slot], kv_buf.at[buf, h], sems.at[buf]).start()

    @pl.when(b == 0)
    def _():
        fetch(0, 0)

    @pl.when(b + 1 < blocks)
    def _():
        fetch(b + 1, (b + 1) % 2)

    cur = b % 2
    pltpu.make_async_copy(kv_buf.at[cur], kv_buf.at[cur], sems.at[cur]).wait()
    rows = group * BS
    dh = q_ref.shape[2]
    weights = []
    tops = []
    totals = []
    for h in range(heads):
        s = lax.dot_general(
            kv_buf[cur, h, 0], q_ref[h], (((1,), (1,)), ((), ())),
            preferred_element_type=jnp.float32,
        )
        top = jnp.max(s, axis=0, keepdims=True)
        p = jnp.exp2((s - top) * (scale * LOG2E))
        weights.append(p)
        tops.append(top)
        totals.append(jnp.sum(p, axis=0, keepdims=True))
    total = jnp.concatenate(totals, axis=0)
    far_lse = jnp.concatenate(tops, axis=0) * scale + jnp.log(total)
    local_lse = lse_ref[0]
    joint = jnp.maximum(local_lse, far_lse)
    head_row = lax.broadcasted_iota(jnp.int32, (heads, 1), 0)
    valid = jnp.zeros((heads, 1), jnp.int32)
    for h in range(heads):
        valid = jnp.where(head_row == h, valid_sm[h * blocks + b], valid)
    a = jnp.where(valid > 0, jnp.exp(local_lse - joint), 1.0)
    c = jnp.where(valid > 0, jnp.exp(far_lse - joint), 0.0)
    local_share = (a / (a + c)).T
    far_share = c / ((a + c) * total)

    low = lax.broadcasted_iota(jnp.int32, (rows // 8, 8, dh), 1) < group
    for quad in range(heads // 4):
        wide = []
        for pair in (2 * quad, 2 * quad + 1):
            halves = []
            for h in (2 * pair, 2 * pair + 1):
                p = (weights[h] * far_share[h : h + 1]).astype(jnp.bfloat16)
                acc = lax.dot_general(
                    p, kv_buf[cur, h, 1], (((0,), (0,)), ((), ())),
                    preferred_element_type=jnp.float32,
                )
                mixed = local_share[:, h : h + 1] * local_ref[h, 0] + acc
                halves.append(mixed.reshape(rows // 8, 8, dh))
            x, y = halves
            even = jnp.where(low, x, pltpu.roll(y, group, 1))
            odd = jnp.where(low, pltpu.roll(x, group, 1), y)
            wide.append(jnp.stack([even, odd], axis=1).reshape(BS, 8, dh))
        both = jnp.concatenate(wide, axis=1)
        out_ref[:, quad * 16 : (quad + 1) * 16, :] = both.astype(jnp.bfloat16)


def vert_pack_kernel(
    rank_sm, vert_sm,
    keys_hbm, values_hbm,
    out_hbm,
    tok_buf, send_buf, sems,
    *, count, verts, blocks, copies,
):
    def look(i, carry):
        head, block = carry
        at = vert_sm[i]
        mine = at // blocks == rank_sm[0]
        return (
            jnp.where(mine, i // verts, head),
            jnp.where(mine, at - rank_sm[0] * blocks, block),
        )

    head, block = lax.fori_loop(0, count, look, (jnp.int32(0), jnp.int32(0)))
    rows = pl.ds(pl.multiple_of(block * BS, BS), BS)
    loads = [
        pltpu.make_async_copy(keys_hbm.at[rows], tok_buf.at[0], sems.at[0]),
        pltpu.make_async_copy(values_hbm.at[rows], tok_buf.at[1], sems.at[1]),
    ]
    for load in loads:
        load.start()
    for which, load in enumerate(loads):
        load.wait()
        tokens = tok_buf[which].astype(jnp.float32)
        here = lax.broadcasted_iota(jnp.int32, tokens.shape, 1) == head
        tile = jnp.sum(jnp.where(here, tokens, 0.0), axis=1).astype(jnp.bfloat16)
        for i in range(which, send_buf.shape[0], 2):
            send_buf[i] = tile
    chunk = send_buf.shape[0]
    stores = [
        pltpu.make_async_copy(send_buf, out_hbm.at[pl.ds(i * chunk, chunk)], sems.at[2 + i])
        for i in range(copies)
    ]
    for store in stores:
        store.start()
    for store in stores:
        store.wait()


def shards(queries, keys, values, vert_blocks, slash_offsets, far_blocks):
    tok, q_heads, dh = queries.shape
    heads = keys.shape[1]
    group = q_heads // heads
    blocks = tok // BS
    verts = vert_blocks.shape[1]
    near = slash_offsets.shape[1]
    reqs = heads * blocks
    devices = lax.axis_size(AXES)
    rank = lax.axis_index(AXES)
    core = rank % 2
    scale = dh**-0.5
    halo_rows = (NW - 1) * BS
    rows = group * BS

    forward = [(i, i + 1) for i in range(devices - 1)]
    halo_k = lax.ppermute(keys[tok - halo_rows :], AXES, forward)
    halo_v = lax.ppermute(values[tok - halo_rows :], AXES, forward)

    copies = 8
    vert_send = pl.pallas_call(
        functools.partial(
            vert_pack_kernel, count=heads * verts, verts=verts, blocks=blocks, copies=copies
        ),
        grid_spec=pltpu.PrefetchScalarGridSpec(
            num_scalar_prefetch=2,
            grid=(1,),
            in_specs=[pl.BlockSpec(memory_space=pl.ANY), pl.BlockSpec(memory_space=pl.ANY)],
            out_specs=pl.BlockSpec(memory_space=pl.ANY),
            scratch_shapes=[
                pltpu.VMEM((2, BS, heads, dh), jnp.bfloat16),
                pltpu.VMEM((devices // copies, BS, dh), jnp.bfloat16),
                pltpu.SemaphoreType.DMA((2 + copies,)),
            ],
        ),
        out_shape=jax.ShapeDtypeStruct((devices, BS, dh), jnp.bfloat16),
        name="vertical_pack",
    )(rank.reshape(1).astype(jnp.int32), vert_blocks.reshape(-1), keys, values)
    vert_send, halo_k = lax.optimization_barrier((vert_send, halo_k))
    vert_mine = lax.all_to_all(vert_send, AXES, split_axis=0, concat_axis=0, tiled=True)

    k_t = keys.transpose(1, 0, 2)
    v_t = values.transpose(1, 0, 2)

    all_far = far_blocks.reshape(heads, devices, blocks).transpose(1, 0, 2).reshape(devices, reqs)
    earlier = (jnp.arange(reqs)[:, None] < jnp.arange(reqs)[None, :]).astype(jnp.float32)
    asked = (all_far >= 0) & (all_far // blocks == rank)
    place = jnp.dot(asked.astype(jnp.float32), earlier).astype(jnp.int32)
    tile = (jnp.arange(reqs)[None, :] // blocks) * blocks + all_far - rank * blocks
    wanted = asked[:, None, :] & (place[:, None, :] == jnp.arange(CAP)[None, :, None])
    send_tile = jnp.max(jnp.where(wanted, tile[:, None, :], 0), axis=2).reshape(-1)
    tiles = jnp.stack(
        [k_t.reshape(heads * blocks, BS, dh), v_t.reshape(heads * blocks, BS, dh)], axis=1
    )
    far_send = tiles[send_tile]
    far_send, vert_mine, halo_k, halo_v = lax.optimization_barrier(
        (far_send, vert_mine, halo_k, halo_v)
    )
    vert_other = lax.ppermute(vert_mine, AXES, [(i, i ^ 1) for i in range(devices)])
    far_send, vert_other = lax.optimization_barrier((far_send, vert_other))
    far_got = lax.all_to_all(far_send, AXES, split_axis=0, concat_axis=0, tiled=True)

    my_far = lax.dynamic_slice_in_dim(far_blocks, rank * blocks, blocks, 1).reshape(-1)
    valid = (my_far >= 0).astype(jnp.int32)
    owner = jnp.where(my_far >= 0, my_far // blocks, -1)
    same = owner[:, None] == owner[None, :]
    my_place = jnp.sum(same & (jnp.arange(reqs)[None, :] < jnp.arange(reqs)[:, None]), axis=1)
    got_slot = jnp.where(my_far >= 0, owner * CAP + jnp.minimum(my_place, CAP - 1), 0)

    q_t = queries.reshape(tok, heads, group, dh).transpose(1, 0, 2, 3).reshape(heads, tok * group, dh)
    zero_at = jnp.argmax((slash_offsets == 0).astype(jnp.int32), axis=1)
    order = (zero_at[:, None] + jnp.arange(near)[None, :]) % near
    offsets = jnp.sum(
        jnp.where(order[:, :, None] == jnp.arange(near)[None, None, :], slash_offsets[:, None, :], 0),
        axis=2,
    )
    my_blocks = rank * blocks + jnp.arange(blocks)
    vert_ok = vert_blocks[:, None, :] <= my_blocks[None, :, None] - NW
    vert_bias = jnp.repeat(jnp.where(vert_ok, 0.0, MASKED).astype(jnp.float32), BS, axis=2)

    by_head = lambda *tail: pl.BlockSpec((1,) + tail, lambda h, *_: (h,) + (0,) * len(tail))
    local_out, local_lse = pl.pallas_call(
        functools.partial(
            local_kernel, heads=heads, verts=verts, blocks=blocks, group=group, near=near,
            scale=scale,
        ),
        grid_spec=pltpu.PrefetchScalarGridSpec(
            num_scalar_prefetch=4,
            grid=(heads,),
            in_specs=[
                by_head(tok * group, dh),
                by_head(tok, dh),
                by_head(tok, dh),
                by_head(halo_rows, dh),
                by_head(halo_rows, dh),
                by_head(blocks, verts * BS),
                pl.BlockSpec(memory_space=pl.ANY),
                pl.BlockSpec(memory_space=pl.ANY),
            ],
            out_specs=[by_head(blocks, rows, dh), by_head(blocks, rows)],
            scratch_shapes=[
                pltpu.VMEM((halo_rows + tok, dh), jnp.bfloat16),
                pltpu.VMEM((halo_rows + tok, dh), jnp.bfloat16),
                pltpu.VMEM((2, verts * BS, dh), jnp.bfloat16),
                pltpu.VMEM((2, verts * BS, dh), jnp.bfloat16),
                pltpu.SemaphoreType.DMA((2, 2)),
            ],
        ),
        out_shape=[
            jax.ShapeDtypeStruct((heads, blocks, rows, dh), jnp.float32),
            jax.ShapeDtypeStruct((heads, blocks, rows), jnp.float32),
        ],
        compiler_params=pltpu.CompilerParams(vmem_limit_bytes=56 * 1024 * 1024),
        cost_estimate=pl.CostEstimate(
            flops=4 * heads * blocks * rows * dh * (near + verts) * BS,
            bytes_accessed=40_000_000,
            transcendentals=heads * blocks * rows * (near + verts) * BS,
        ),
        name="local_attention",
    )(
        core.reshape(1).astype(jnp.int32),
        (vert_blocks // blocks).astype(jnp.int32),
        offsets.astype(jnp.int32),
        (rank * blocks).reshape(1).astype(jnp.int32),
        q_t, k_t, v_t, halo_k.transpose(1, 0, 2), halo_v.transpose(1, 0, 2), vert_bias, vert_mine, vert_other,
    )

    return pl.pallas_call(
        functools.partial(merge_kernel, heads=heads, blocks=blocks, group=group, scale=scale),
        grid_spec=pltpu.PrefetchScalarGridSpec(
            num_scalar_prefetch=2,
            grid=(blocks,),
            in_specs=[
                pl.BlockSpec((heads, rows, dh), lambda b, *_: (0, b, 0)),
                pl.BlockSpec((heads, 1, rows, dh), lambda b, *_: (0, b, 0, 0)),
                pl.BlockSpec((1, heads, rows), lambda b, *_: (b, 0, 0)),
                pl.BlockSpec(memory_space=pl.ANY),
            ],
            out_specs=pl.BlockSpec((BS, q_heads, dh), lambda b, *_: (b, 0, 0)),
            scratch_shapes=[
                pltpu.VMEM((2, heads, 2, BS, dh), jnp.bfloat16),
                pltpu.SemaphoreType.DMA((2,)),
            ],
        ),
        out_shape=jax.ShapeDtypeStruct((tok, q_heads, dh), jnp.bfloat16),
        compiler_params=pltpu.CompilerParams(vmem_limit_bytes=56 * 1024 * 1024),
        cost_estimate=pl.CostEstimate(
            flops=4 * heads * blocks * rows * dh * BS,
            bytes_accessed=25_000_000,
            transcendentals=heads * blocks * rows * BS,
        ),
        name="far_merge",
    )(got_slot.astype(jnp.int32), valid, q_t, local_out, local_lse.transpose(1, 0, 2), far_got)


def solution(mesh):
    split = P(AXES, None, None)
    return jax.shard_map(
        shards,
        mesh=mesh,
        in_specs=(split, split, split, P(), P(), P()),
        out_specs=split,
        check_vma=False,
    )
```

```python
import functools

import jax
import jax.numpy as jnp
from jax import lax
from jax.experimental import pallas as pl
from jax.experimental.pallas import tpu as pltpu
from jax.sharding import PartitionSpec as P

BS = 64
NW = 8
CAP = 2
AXES = ("blk", "grid")
MASKED = -1e30
LOG2E = 1.4426950408889634


def local_kernel(
    core_sm, slot_sm, off_sm, first_sm,
    q_ref, ko_ref, vo_ref, kh_ref, vh_ref, bias_ref, mine_hbm, other_hbm,
    out_ref, lse_ref,
    kx, vx, kv_buf, vv_buf, lse_buf, sems,
    *, heads, verts, blocks, group, near, scale,
):
    h = pl.program_id(0)
    halo = kh_ref.shape[1]
    own = ko_ref.shape[1]
    dh = q_ref.shape[2]
    left = pl.ds(0, dh)

    def fetch(head, buf):
        def copies(k_from, v_from):
            for i in range(verts):
                slot = slot_sm[head, i]
                rows = pl.ds(i * BS, BS)
                pltpu.make_async_copy(
                    k_from(slot), kv_buf.at[buf, rows], sems.at[buf, 0]
                ).start()
                pltpu.make_async_copy(
                    v_from(slot), vv_buf.at[buf, rows, left], sems.at[buf, 1]
                ).start()

        mine = lambda slot: mine_hbm.at[slot, 2]
        other = lambda slot: other_hbm.at[slot]

        @pl.when(core_sm[0] == 0)
        def _():
            copies(mine, other)

        @pl.when(core_sm[0] != 0)
        def _():
            copies(other, mine)

    @pl.when(h == 0)
    def _():
        vx[:, dh:] = jnp.ones((halo + own, dh), jnp.bfloat16)
        for buf in range(2):
            vv_buf[buf, :, dh:] = jnp.ones((verts * BS, dh), jnp.bfloat16)
        fetch(0, 0)

    @pl.when(h + 1 < heads)
    def _():
        fetch(h + 1, (h + 1) % 2)

    kx[0:halo] = kh_ref[0]
    kx[halo : halo + own] = ko_ref[0]
    vx[0:halo, :dh] = vh_ref[0]
    vx[halo : halo + own, :dh] = vo_ref[0]
    cur = h % 2
    pltpu.make_async_copy(kv_buf.at[cur], kv_buf.at[cur], sems.at[cur, 0]).wait()
    pltpu.make_async_copy(
        vv_buf.at[cur, :, left], vv_buf.at[cur, :, left], sems.at[cur, 1]
    ).wait()

    t_pos = lax.broadcasted_iota(jnp.int32, (group * BS, near * BS), 0) // group
    u_pos = lax.broadcasted_iota(jnp.int32, (group * BS, near * BS), 1)
    causal_bias = jnp.where((u_pos < BS) & (u_pos > t_pos), MASKED, 0.0)
    lane = lax.broadcasted_iota(jnp.int32, (1, near * BS), 1) // BS

    def one_block(b, carry):
        rows = pl.multiple_of(b * group * BS, group * BS)
        q = q_ref[0, pl.ds(rows, group * BS), :]
        k_parts = []
        v_parts = []
        row_bias = jnp.zeros((1, near * BS), jnp.float32)
        for i in range(near):
            off = off_sm[h, i]
            start = pl.multiple_of((b + NW - 1 - off) * BS, BS)
            k_parts.append(kx[pl.ds(start, BS), :])
            v_parts.append(vx[pl.ds(start, BS), :])
            miss = jnp.where(first_sm[0] + b < off, MASKED, 0.0)
            row_bias = jnp.where(lane == i, miss, row_bias)
        k_near = jnp.concatenate(k_parts, axis=0)
        v_near = jnp.concatenate(v_parts, axis=0)
        dims = (((1,), (1,)), ((), ()))
        s_near = lax.dot_general(q, k_near, dims, preferred_element_type=jnp.float32)
        s_near = s_near + (causal_bias + row_bias)
        s_vert = lax.dot_general(q, kv_buf[cur], dims, preferred_element_type=jnp.float32)
        s_vert = s_vert + bias_ref[0, pl.ds(b, 1), :]
        top = jnp.maximum(
            jnp.max(s_near, axis=1, keepdims=True), jnp.max(s_vert, axis=1, keepdims=True)
        )
        p_near = jnp.exp2((s_near - top) * (scale * LOG2E)).astype(jnp.bfloat16)
        p_vert = jnp.exp2((s_vert - top) * (scale * LOG2E)).astype(jnp.bfloat16)
        acc = jnp.dot(p_near, v_near, preferred_element_type=jnp.float32)
        acc = acc + jnp.dot(p_vert, vv_buf[cur], preferred_element_type=jnp.float32)
        total = acc[:, dh:]
        out_ref[0, b] = acc[:, :dh] / total
        column = lax.broadcasted_iota(jnp.int32, total.shape, 1) == b
        lse_buf[...] = jnp.where(column, top * scale + jnp.log(total), lse_buf[...])
        return carry

    lax.fori_loop(0, blocks, one_block, 0, unroll=True)
    lse_ref[0] = lse_buf[...].T[:blocks]


def pack_kernel(tile_sm, vert_sm, k_ref, v_ref, out_ref):
    base = pl.program_id(0) * out_ref.shape[0]
    for d in range(out_ref.shape[0]):
        tile = tile_sm[base + d]
        out_ref[d, 0] = k_ref[tile]
        out_ref[d, 1] = v_ref[tile]
        out_ref[d, 2] = (v_ref if d % 2 else k_ref)[vert_sm[0]]


def merge_kernel(
    owner_sm, place_sm, valid_sm,
    q_ref, local_ref, lse_ref, first_hbm, second_hbm,
    out_ref,
    kv_buf, sems,
    *, heads, blocks, group, per, scale,
):
    step = pl.program_id(0)

    def fetch(at, buf):
        for j in range(per):
            for h in range(heads):
                request = h * blocks + at * per + j
                owner = owner_sm[request]
                to = kv_buf.at[buf, j, h]

                @pl.when(place_sm[request] == 0)
                def _():
                    pltpu.make_async_copy(
                        first_hbm.at[owner, pl.ds(0, 2)], to, sems.at[buf]
                    ).start()

                @pl.when(place_sm[request] != 0)
                def _():
                    pltpu.make_async_copy(second_hbm.at[owner], to, sems.at[buf]).start()

    @pl.when(step == 0)
    def _():
        fetch(0, 0)

    @pl.when(step + 1 < blocks // per)
    def _():
        fetch(step + 1, (step + 1) % 2)

    cur = step % 2
    pltpu.make_async_copy(kv_buf.at[cur], kv_buf.at[cur], sems.at[cur]).wait()
    rows = group * BS
    dh = q_ref.shape[2]
    head_row = lax.broadcasted_iota(jnp.int32, (heads, 1), 0)
    low = lax.broadcasted_iota(jnp.int32, (rows // 8, 8, dh), 1) < group
    for j in range(per):
        weights = []
        tops = []
        totals = []
        for h in range(heads):
            s = lax.dot_general(
                kv_buf[cur, j, h, 0], q_ref[h, j * rows : (j + 1) * rows, :],
                (((1,), (1,)), ((), ())), preferred_element_type=jnp.float32,
            )
            top = jnp.max(s, axis=0, keepdims=True)
            p = jnp.exp2((s - top) * (scale * LOG2E))
            weights.append(p)
            tops.append(top)
            totals.append(jnp.sum(p, axis=0, keepdims=True))
        total = jnp.concatenate(totals, axis=0)
        far_lse = jnp.concatenate(tops, axis=0) * scale + jnp.log(total)
        local_lse = lse_ref[j]
        joint = jnp.maximum(local_lse, far_lse)
        valid = jnp.zeros((heads, 1), jnp.int32)
        for h in range(heads):
            valid = jnp.where(head_row == h, valid_sm[h * blocks + step * per + j], valid)
        a = jnp.where(valid > 0, jnp.exp(local_lse - joint), 1.0)
        c = jnp.where(valid > 0, jnp.exp(far_lse - joint), 0.0)
        local_share = (a / (a + c)).T
        far_share = c / ((a + c) * total)

        for quad in range(heads // 4):
            wide = []
            for pair in (2 * quad, 2 * quad + 1):
                halves = []
                for h in (2 * pair, 2 * pair + 1):
                    p = (weights[h] * far_share[h : h + 1]).astype(jnp.bfloat16)
                    acc = lax.dot_general(
                        p, kv_buf[cur, j, h, 1], (((0,), (0,)), ((), ())),
                        preferred_element_type=jnp.float32,
                    )
                    mixed = local_share[:, h : h + 1] * local_ref[h, j] + acc
                    halves.append(mixed.reshape(rows // 8, 8, dh))
                x, y = halves
                even = jnp.where(low, x, pltpu.roll(y, group, 1))
                odd = jnp.where(low, pltpu.roll(x, group, 1), y)
                wide.append(jnp.stack([even, odd], axis=1).reshape(BS, 8, dh))
            both = jnp.concatenate(wide, axis=1)
            out_ref[j * BS : (j + 1) * BS, quad * 16 : (quad + 1) * 16, :] = both.astype(
                jnp.bfloat16
            )


def shards(queries, keys, values, vert_blocks, slash_offsets, far_blocks):
    tok, q_heads, dh = queries.shape
    heads = keys.shape[1]
    group = q_heads // heads
    blocks = tok // BS
    verts = vert_blocks.shape[1]
    near = slash_offsets.shape[1]
    reqs = heads * blocks
    devices = lax.axis_size(AXES)
    rank = lax.axis_index(AXES)
    core = rank % 2
    scale = dh**-0.5
    halo_rows = (NW - 1) * BS
    rows = group * BS

    forward = [(i, i + 1) for i in range(devices - 1)]
    halo_k = lax.ppermute(keys[tok - halo_rows :], AXES, forward)
    halo_v = lax.ppermute(values[tok - halo_rows :], AXES, forward)

    k_t = keys.transpose(1, 0, 2)
    v_t = values.transpose(1, 0, 2)
    tiles = jnp.concatenate(
        [k_t.reshape(reqs, BS, dh), v_t.reshape(reqs, BS, dh)], axis=0
    )

    vert_here = vert_blocks - rank * blocks
    vert_tile = jnp.max(
        jnp.where(
            (vert_here >= 0) & (vert_here < blocks),
            vert_here + jnp.arange(heads)[:, None] * blocks,
            0,
        )
    )

    all_far = far_blocks.reshape(heads, devices, blocks).transpose(1, 0, 2).reshape(devices, reqs)
    earlier = (jnp.arange(reqs)[:, None] < jnp.arange(reqs)[None, :]).astype(jnp.float32)
    asked = (all_far >= 0) & (all_far // blocks == rank)
    place = jnp.dot(asked.astype(jnp.float32), earlier).astype(jnp.int32)
    tile = (jnp.arange(reqs)[None, :] // blocks) * blocks + all_far - rank * blocks
    wanted = asked[:, None, :] & (place[:, None, :] == jnp.arange(CAP)[None, :, None])
    send_tile = jnp.max(jnp.where(wanted, tile[:, None, :], 0), axis=2)
    second = send_tile[:, 1:]
    chunk = 16
    whole = pl.BlockSpec((reqs, BS, dh), lambda i, *_: (0, 0, 0))
    first_send = pl.pallas_call(
        pack_kernel,
        grid_spec=pltpu.PrefetchScalarGridSpec(
            num_scalar_prefetch=2,
            grid=(devices // chunk,),
            in_specs=[whole, whole],
            out_specs=pl.BlockSpec((chunk, 3, BS, dh), lambda i, *_: (i, 0, 0, 0)),
        ),
        out_shape=jax.ShapeDtypeStruct((devices, 3, BS, dh), jnp.bfloat16),
        compiler_params=pltpu.CompilerParams(vmem_limit_bytes=32 * 1024 * 1024),
        name="pack_first",
    )(
        send_tile[:, 0], vert_tile.reshape(1),
        k_t.reshape(reqs, BS, dh), v_t.reshape(reqs, BS, dh),
    )
    first_send, halo_k = lax.optimization_barrier((first_send, halo_k))
    first_got = lax.all_to_all(first_send, AXES, split_axis=0, concat_axis=0, tiled=True)
    second_send = tiles[jnp.concatenate([second, second + reqs], axis=1)]
    my_far = lax.dynamic_slice_in_dim(far_blocks, rank * blocks, blocks, 1).reshape(-1)
    valid = (my_far >= 0).astype(jnp.int32)
    owner = jnp.where(my_far >= 0, my_far // blocks, -1)
    same = owner[:, None] == owner[None, :]
    my_place = jnp.sum(same & (jnp.arange(reqs)[None, :] < jnp.arange(reqs)[:, None]), axis=1)

    q_t = queries.reshape(tok, heads, group, dh).transpose(1, 0, 2, 3).reshape(heads, tok * group, dh)
    zero_at = jnp.argmax((slash_offsets == 0).astype(jnp.int32), axis=1)
    order = (zero_at[:, None] + jnp.arange(near)[None, :]) % near
    offsets = jnp.sum(
        jnp.where(order[:, :, None] == jnp.arange(near)[None, None, :], slash_offsets[:, None, :], 0),
        axis=2,
    )
    my_blocks = rank * blocks + jnp.arange(blocks)
    vert_ok = vert_blocks[:, None, :] <= my_blocks[None, :, None] - NW
    vert_bias = jnp.repeat(jnp.where(vert_ok, 0.0, MASKED).astype(jnp.float32), BS, axis=2)

    owner_at = jnp.maximum(owner, 0).astype(jnp.int32)
    my_place = my_place.astype(jnp.int32)
    offsets = offsets.astype(jnp.int32)
    second_send, first_got, halo_k, halo_v, q_t, vert_bias, offsets, owner_at, my_place, valid = (
        lax.optimization_barrier(
            (
                second_send, first_got, halo_k, halo_v,
                q_t, vert_bias, offsets, owner_at, my_place, valid,
            )
        )
    )
    vert_other = lax.ppermute(first_got[:, 2], AXES, [(i, i ^ 1) for i in range(devices)])
    second_send, vert_other = lax.optimization_barrier((second_send, vert_other))
    second_got = lax.all_to_all(second_send, AXES, split_axis=0, concat_axis=0, tiled=True)

    by_head = lambda *tail: pl.BlockSpec((1,) + tail, lambda h, *_: (h,) + (0,) * len(tail))
    local_out, local_lse = pl.pallas_call(
        functools.partial(
            local_kernel, heads=heads, verts=verts, blocks=blocks, group=group, near=near,
            scale=scale,
        ),
        grid_spec=pltpu.PrefetchScalarGridSpec(
            num_scalar_prefetch=4,
            grid=(heads,),
            in_specs=[
                by_head(tok * group, dh),
                by_head(tok, dh),
                by_head(tok, dh),
                by_head(halo_rows, dh),
                by_head(halo_rows, dh),
                by_head(blocks, verts * BS),
                pl.BlockSpec(memory_space=pltpu.HBM),
                pl.BlockSpec(memory_space=pltpu.HBM),
            ],
            out_specs=[by_head(blocks, rows, dh), by_head(blocks, rows)],
            scratch_shapes=[
                pltpu.VMEM((halo_rows + tok, dh), jnp.bfloat16),
                pltpu.VMEM((halo_rows + tok, 2 * dh), jnp.bfloat16),
                pltpu.VMEM((2, verts * BS, dh), jnp.bfloat16),
                pltpu.VMEM((2, verts * BS, 2 * dh), jnp.bfloat16),
                pltpu.VMEM((rows, 128), jnp.float32),
                pltpu.SemaphoreType.DMA((2, 2)),
            ],
        ),
        out_shape=[
            jax.ShapeDtypeStruct((heads, blocks, rows, dh), jnp.float32),
            jax.ShapeDtypeStruct((heads, blocks, rows), jnp.float32),
        ],
        compiler_params=pltpu.CompilerParams(vmem_limit_bytes=56 * 1024 * 1024),
        cost_estimate=pl.CostEstimate(
            flops=4 * heads * blocks * rows * dh * (near + verts) * BS,
            bytes_accessed=40_000_000,
            transcendentals=heads * blocks * rows * (near + verts) * BS,
        ),
        name="local_attention",
    )(
        core.reshape(1).astype(jnp.int32),
        (vert_blocks // blocks).astype(jnp.int32),
        offsets,
        (rank * blocks).reshape(1).astype(jnp.int32),
        q_t, k_t, v_t, halo_k.transpose(1, 0, 2), halo_v.transpose(1, 0, 2), vert_bias, first_got, vert_other,
    )

    per = 2 if blocks % 2 == 0 else 1
    return pl.pallas_call(
        functools.partial(
            merge_kernel, heads=heads, blocks=blocks, group=group, per=per, scale=scale
        ),
        grid_spec=pltpu.PrefetchScalarGridSpec(
            num_scalar_prefetch=3,
            grid=(blocks // per,),
            in_specs=[
                pl.BlockSpec((heads, per * rows, dh), lambda b, *_: (0, b, 0)),
                pl.BlockSpec((heads, per, rows, dh), lambda b, *_: (0, b, 0, 0)),
                pl.BlockSpec((per, heads, rows), lambda b, *_: (b, 0, 0)),
                pl.BlockSpec(memory_space=pl.ANY),
                pl.BlockSpec(memory_space=pl.ANY),
            ],
            out_specs=pl.BlockSpec((per * BS, q_heads, dh), lambda b, *_: (b, 0, 0)),
            scratch_shapes=[
                pltpu.VMEM((2, per, heads, 2, BS, dh), jnp.bfloat16),
                pltpu.SemaphoreType.DMA((2,)),
            ],
        ),
        out_shape=jax.ShapeDtypeStruct((tok, q_heads, dh), jnp.bfloat16),
        compiler_params=pltpu.CompilerParams(vmem_limit_bytes=56 * 1024 * 1024),
        cost_estimate=pl.CostEstimate(
            flops=4 * heads * blocks * rows * dh * BS,
            bytes_accessed=25_000_000,
            transcendentals=heads * blocks * rows * BS,
        ),
        name="far_merge",
    )(
        owner_at, my_place, valid,
        q_t, local_out, local_lse.transpose(1, 0, 2), first_got, second_got,
    )


def solution(mesh):
    split = P(AXES, None, None)
    return jax.shard_map(
        shards,
        mesh=mesh,
        in_specs=(split, split, split, P(), P(), P()),
        out_specs=split,
        check_vma=False,
    )
```

```python
import functools

import jax
import jax.numpy as jnp
from jax import lax
from jax.experimental import pallas as pl
from jax.experimental.pallas import tpu as pltpu
from jax.sharding import PartitionSpec as P

BS = 64
NW = 8
CAP = 2
AXES = ("blk", "grid")
MASKED = -1e30
LOG2E = 1.4426950408889634


def local_kernel(
    core_sm, slot_sm, off_sm, first_sm,
    q_ref, ko_ref, vo_ref, kh_ref, vh_ref, bias_ref, mine_hbm, other_hbm,
    out_ref, lse_ref,
    kx, vx, kv_buf, vv_buf, lse_buf, sems,
    *, heads, verts, blocks, group, near, scale,
):
    h = pl.program_id(0)
    halo = kh_ref.shape[1]
    own = ko_ref.shape[1]
    dh = q_ref.shape[2]
    left = pl.ds(0, dh)

    def fetch(head, buf):
        def copies(k_from, v_from):
            for i in range(verts):
                slot = slot_sm[head, i]
                rows = pl.ds(i * BS, BS)
                pltpu.make_async_copy(
                    k_from(slot), kv_buf.at[buf, rows], sems.at[buf, 0]
                ).start()
                pltpu.make_async_copy(
                    v_from(slot), vv_buf.at[buf, rows, left], sems.at[buf, 1]
                ).start()

        mine = lambda slot: mine_hbm.at[slot, 2]
        other = lambda slot: other_hbm.at[slot]

        @pl.when(core_sm[0] == 0)
        def _():
            copies(mine, other)

        @pl.when(core_sm[0] != 0)
        def _():
            copies(other, mine)

    @pl.when(h == 0)
    def _():
        vx[:, dh:] = jnp.ones((halo + own, dh), jnp.bfloat16)
        for buf in range(2):
            vv_buf[buf, :, dh:] = jnp.ones((verts * BS, dh), jnp.bfloat16)
        fetch(0, 0)

    @pl.when(h + 1 < heads)
    def _():
        fetch(h + 1, (h + 1) % 2)

    kx[0:halo] = kh_ref[0]
    kx[halo : halo + own] = ko_ref[0]
    vx[0:halo, :dh] = vh_ref[0]
    vx[halo : halo + own, :dh] = vo_ref[0]
    cur = h % 2
    pltpu.make_async_copy(kv_buf.at[cur], kv_buf.at[cur], sems.at[cur, 0]).wait()
    pltpu.make_async_copy(
        vv_buf.at[cur, :, left], vv_buf.at[cur, :, left], sems.at[cur, 1]
    ).wait()

    t_pos = lax.broadcasted_iota(jnp.int32, (group * BS, near * BS), 0) // group
    u_pos = lax.broadcasted_iota(jnp.int32, (group * BS, near * BS), 1)
    causal_bias = jnp.where((u_pos < BS) & (u_pos > t_pos), MASKED, 0.0)
    lane = lax.broadcasted_iota(jnp.int32, (1, near * BS), 1) // BS

    def one_block(b, carry):
        rows = pl.multiple_of(b * group * BS, group * BS)
        q = q_ref[0, pl.ds(rows, group * BS), :]
        k_parts = []
        v_parts = []
        row_bias = jnp.zeros((1, near * BS), jnp.float32)
        for i in range(near):
            off = off_sm[h, i]
            start = pl.multiple_of((b + NW - 1 - off) * BS, BS)
            k_parts.append(kx[pl.ds(start, BS), :])
            v_parts.append(vx[pl.ds(start, BS), :])
            miss = jnp.where(first_sm[0] + b < off, MASKED, 0.0)
            row_bias = jnp.where(lane == i, miss, row_bias)
        k_near = jnp.concatenate(k_parts, axis=0)
        v_near = jnp.concatenate(v_parts, axis=0)
        dims = (((1,), (1,)), ((), ()))
        s_near = lax.dot_general(q, k_near, dims, preferred_element_type=jnp.float32)
        s_near = s_near + (causal_bias + row_bias)
        s_vert = lax.dot_general(q, kv_buf[cur], dims, preferred_element_type=jnp.float32)
        s_vert = s_vert + bias_ref[0, pl.ds(b, 1), :]
        top = jnp.maximum(
            jnp.max(s_near, axis=1, keepdims=True), jnp.max(s_vert, axis=1, keepdims=True)
        )
        p_near = jnp.exp2((s_near - top) * (scale * LOG2E)).astype(jnp.bfloat16)
        p_vert = jnp.exp2((s_vert - top) * (scale * LOG2E)).astype(jnp.bfloat16)
        acc = jnp.dot(p_near, v_near, preferred_element_type=jnp.float32)
        acc = acc + jnp.dot(p_vert, vv_buf[cur], preferred_element_type=jnp.float32)
        total = acc[:, dh:]
        out_ref[0, b] = acc[:, :dh] / total
        column = lax.broadcasted_iota(jnp.int32, total.shape, 1) == b
        lse_buf[...] = jnp.where(column, top * scale + jnp.log(total), lse_buf[...])
        return carry

    lax.fori_loop(0, blocks, one_block, 0, unroll=True)
    lse_ref[0] = lse_buf[...].T[:blocks]


def pack_kernel(tile_sm, vert_sm, k_ref, v_ref, out_ref):
    base = pl.program_id(0) * out_ref.shape[0]
    for d in range(out_ref.shape[0]):
        tile = tile_sm[base + d]
        out_ref[d, 0] = k_ref[tile]
        out_ref[d, 1] = v_ref[tile]
        out_ref[d, 2] = (v_ref if d % 2 else k_ref)[vert_sm[0]]


def pack_second_kernel(tile_sm, k_ref, v_ref, out_ref):
    base = pl.program_id(0) * out_ref.shape[0]
    for d in range(out_ref.shape[0]):
        tile = tile_sm[base + d]
        out_ref[d, 0] = k_ref[tile]
        out_ref[d, 1] = v_ref[tile]


def merge_kernel(
    owner_sm, place_sm, valid_sm,
    q_ref, local_ref, lse_ref, first_hbm, second_hbm,
    out_ref,
    kv_buf, sems,
    *, heads, blocks, group, per, scale,
):
    step = pl.program_id(0)

    def fetch(at, buf):
        for j in range(per):
            for h in range(heads):
                request = h * blocks + at * per + j
                owner = owner_sm[request]
                to = kv_buf.at[buf, j, h]

                @pl.when(place_sm[request] == 0)
                def _():
                    pltpu.make_async_copy(
                        first_hbm.at[owner, pl.ds(0, 2)], to, sems.at[buf]
                    ).start()

                @pl.when(place_sm[request] != 0)
                def _():
                    pltpu.make_async_copy(second_hbm.at[owner], to, sems.at[buf]).start()

    @pl.when(step == 0)
    def _():
        fetch(0, 0)

    @pl.when(step + 1 < blocks // per)
    def _():
        fetch(step + 1, (step + 1) % 2)

    cur = step % 2
    pltpu.make_async_copy(kv_buf.at[cur], kv_buf.at[cur], sems.at[cur]).wait()
    rows = group * BS
    dh = q_ref.shape[2]
    head_row = lax.broadcasted_iota(jnp.int32, (heads, 1), 0)
    low = lax.broadcasted_iota(jnp.int32, (rows // 8, 8, dh), 1) < group
    for j in range(per):
        weights = []
        tops = []
        totals = []
        for h in range(heads):
            s = lax.dot_general(
                kv_buf[cur, j, h, 0], q_ref[h, j * rows : (j + 1) * rows, :],
                (((1,), (1,)), ((), ())), preferred_element_type=jnp.float32,
            )
            top = jnp.max(s, axis=0, keepdims=True)
            p = jnp.exp2((s - top) * (scale * LOG2E))
            weights.append(p)
            tops.append(top)
            totals.append(jnp.sum(p, axis=0, keepdims=True))
        total = jnp.concatenate(totals, axis=0)
        far_lse = jnp.concatenate(tops, axis=0) * scale + jnp.log(total)
        local_lse = lse_ref[j]
        joint = jnp.maximum(local_lse, far_lse)
        valid = jnp.zeros((heads, 1), jnp.int32)
        for h in range(heads):
            valid = jnp.where(head_row == h, valid_sm[h * blocks + step * per + j], valid)
        a = jnp.where(valid > 0, jnp.exp(local_lse - joint), 1.0)
        c = jnp.where(valid > 0, jnp.exp(far_lse - joint), 0.0)
        local_share = (a / (a + c)).T
        far_share = c / ((a + c) * total)

        for quad in range(heads // 4):
            wide = []
            for pair in (2 * quad, 2 * quad + 1):
                halves = []
                for h in (2 * pair, 2 * pair + 1):
                    p = (weights[h] * far_share[h : h + 1]).astype(jnp.bfloat16)
                    acc = lax.dot_general(
                        p, kv_buf[cur, j, h, 1], (((0,), (0,)), ((), ())),
                        preferred_element_type=jnp.float32,
                    )
                    mixed = local_share[:, h : h + 1] * local_ref[h, j] + acc
                    halves.append(mixed.reshape(rows // 8, 8, dh))
                x, y = halves
                even = jnp.where(low, x, pltpu.roll(y, group, 1))
                odd = jnp.where(low, pltpu.roll(x, group, 1), y)
                wide.append(jnp.stack([even, odd], axis=1).reshape(BS, 8, dh))
            both = jnp.concatenate(wide, axis=1)
            out_ref[j * BS : (j + 1) * BS, quad * 16 : (quad + 1) * 16, :] = both.astype(
                jnp.bfloat16
            )


def shards(queries, keys, values, vert_blocks, slash_offsets, far_blocks):
    tok, q_heads, dh = queries.shape
    heads = keys.shape[1]
    group = q_heads // heads
    blocks = tok // BS
    verts = vert_blocks.shape[1]
    near = slash_offsets.shape[1]
    reqs = heads * blocks
    devices = lax.axis_size(AXES)
    rank = lax.axis_index(AXES)
    core = rank % 2
    scale = dh**-0.5
    halo_rows = (NW - 1) * BS
    rows = group * BS

    forward = [(i, i + 1) for i in range(devices - 1)]
    halo_k = lax.ppermute(keys[tok - halo_rows :], AXES, forward)
    halo_v = lax.ppermute(values[tok - halo_rows :], AXES, forward)

    k_t = keys.transpose(1, 0, 2)
    v_t = values.transpose(1, 0, 2)

    vert_here = vert_blocks - rank * blocks
    vert_tile = jnp.max(
        jnp.where(
            (vert_here >= 0) & (vert_here < blocks),
            vert_here + jnp.arange(heads)[:, None] * blocks,
            0,
        )
    )

    all_far = far_blocks.reshape(heads, devices, blocks).transpose(1, 0, 2).reshape(devices, reqs)
    earlier = (jnp.arange(reqs)[:, None] < jnp.arange(reqs)[None, :]).astype(jnp.float32)
    asked = (all_far >= 0) & (all_far // blocks == rank)
    place = jnp.dot(asked.astype(jnp.float32), earlier).astype(jnp.int32)
    tile = (jnp.arange(reqs)[None, :] // blocks) * blocks + all_far - rank * blocks
    wanted = asked[:, None, :] & (place[:, None, :] == jnp.arange(CAP)[None, :, None])
    send_tile = jnp.max(jnp.where(wanted, tile[:, None, :], 0), axis=2)
    chunk = 16
    whole = pl.BlockSpec((reqs, BS, dh), lambda i, *_: (0, 0, 0))
    first_send = pl.pallas_call(
        pack_kernel,
        grid_spec=pltpu.PrefetchScalarGridSpec(
            num_scalar_prefetch=2,
            grid=(devices // chunk,),
            in_specs=[whole, whole],
            out_specs=pl.BlockSpec((chunk, 3, BS, dh), lambda i, *_: (i, 0, 0, 0)),
        ),
        out_shape=jax.ShapeDtypeStruct((devices, 3, BS, dh), jnp.bfloat16),
        compiler_params=pltpu.CompilerParams(vmem_limit_bytes=32 * 1024 * 1024),
        name="pack_first",
    )(
        send_tile[:, 0], vert_tile.reshape(1),
        k_t.reshape(reqs, BS, dh), v_t.reshape(reqs, BS, dh),
    )
    first_got = lax.all_to_all(first_send, AXES, split_axis=0, concat_axis=0, tiled=True)
    second, halo_k, halo_v = lax.optimization_barrier((send_tile[:, 1], halo_k, halo_v))
    second_send = pl.pallas_call(
        pack_second_kernel,
        grid_spec=pltpu.PrefetchScalarGridSpec(
            num_scalar_prefetch=1,
            grid=(devices // chunk,),
            in_specs=[whole, whole],
            out_specs=pl.BlockSpec((chunk, 2, BS, dh), lambda i, *_: (i, 0, 0, 0)),
        ),
        out_shape=jax.ShapeDtypeStruct((devices, 2, BS, dh), jnp.bfloat16),
        compiler_params=pltpu.CompilerParams(vmem_limit_bytes=32 * 1024 * 1024),
        cost_estimate=pl.CostEstimate(
            flops=10**12, bytes_accessed=6_000_000, transcendentals=0
        ),
        name="pack_second",
    )(second, k_t.reshape(reqs, BS, dh), v_t.reshape(reqs, BS, dh))
    my_far = lax.dynamic_slice_in_dim(far_blocks, rank * blocks, blocks, 1).reshape(-1)
    valid = (my_far >= 0).astype(jnp.int32)
    owner = jnp.where(my_far >= 0, my_far // blocks, -1)
    same = owner[:, None] == owner[None, :]
    my_place = jnp.sum(same & (jnp.arange(reqs)[None, :] < jnp.arange(reqs)[:, None]), axis=1)

    q_t = queries.reshape(tok, heads, group, dh).transpose(1, 0, 2, 3).reshape(heads, tok * group, dh)
    zero_at = jnp.argmax((slash_offsets == 0).astype(jnp.int32), axis=1)
    order = (zero_at[:, None] + jnp.arange(near)[None, :]) % near
    offsets = jnp.sum(
        jnp.where(order[:, :, None] == jnp.arange(near)[None, None, :], slash_offsets[:, None, :], 0),
        axis=2,
    )
    my_blocks = rank * blocks + jnp.arange(blocks)
    vert_ok = vert_blocks[:, None, :] <= my_blocks[None, :, None] - NW
    vert_bias = jnp.repeat(jnp.where(vert_ok, 0.0, MASKED).astype(jnp.float32), BS, axis=2)

    owner_at = jnp.maximum(owner, 0).astype(jnp.int32)
    my_place = my_place.astype(jnp.int32)
    offsets = offsets.astype(jnp.int32)
    second_send, first_got, halo_k, halo_v, q_t, vert_bias, offsets, owner_at, my_place, valid = (
        lax.optimization_barrier(
            (
                second_send, first_got, halo_k, halo_v,
                q_t, vert_bias, offsets, owner_at, my_place, valid,
            )
        )
    )
    vert_other = lax.ppermute(first_got[:, 2], AXES, [(i, i ^ 1) for i in range(devices)])
    second_got = lax.all_to_all(second_send, AXES, split_axis=0, concat_axis=0, tiled=True)

    by_head = lambda *tail: pl.BlockSpec((1,) + tail, lambda h, *_: (h,) + (0,) * len(tail))
    local_out, local_lse = pl.pallas_call(
        functools.partial(
            local_kernel, heads=heads, verts=verts, blocks=blocks, group=group, near=near,
            scale=scale,
        ),
        grid_spec=pltpu.PrefetchScalarGridSpec(
            num_scalar_prefetch=4,
            grid=(heads,),
            in_specs=[
                by_head(tok * group, dh),
                by_head(tok, dh),
                by_head(tok, dh),
                by_head(halo_rows, dh),
                by_head(halo_rows, dh),
                by_head(blocks, verts * BS),
                pl.BlockSpec(memory_space=pltpu.HBM),
                pl.BlockSpec(memory_space=pltpu.HBM),
            ],
            out_specs=[by_head(blocks, rows, dh), by_head(blocks, rows)],
            scratch_shapes=[
                pltpu.VMEM((halo_rows + tok, dh), jnp.bfloat16),
                pltpu.VMEM((halo_rows + tok, 2 * dh), jnp.bfloat16),
                pltpu.VMEM((2, verts * BS, dh), jnp.bfloat16),
                pltpu.VMEM((2, verts * BS, 2 * dh), jnp.bfloat16),
                pltpu.VMEM((rows, 128), jnp.float32),
                pltpu.SemaphoreType.DMA((2, 2)),
            ],
        ),
        out_shape=[
            jax.ShapeDtypeStruct((heads, blocks, rows, dh), jnp.float32),
            jax.ShapeDtypeStruct((heads, blocks, rows), jnp.float32),
        ],
        compiler_params=pltpu.CompilerParams(vmem_limit_bytes=56 * 1024 * 1024),
        cost_estimate=pl.CostEstimate(
            flops=400 * heads * blocks * rows * dh * (near + verts) * BS,
            bytes_accessed=40_000_000,
            transcendentals=heads * blocks * rows * (near + verts) * BS,
        ),
        name="local_attention",
    )(
        core.reshape(1).astype(jnp.int32),
        (vert_blocks // blocks).astype(jnp.int32),
        offsets,
        (rank * blocks).reshape(1).astype(jnp.int32),
        q_t, k_t, v_t, halo_k.transpose(1, 0, 2), halo_v.transpose(1, 0, 2), vert_bias, first_got, vert_other,
    )

    per = 2 if blocks % 2 == 0 else 1
    return pl.pallas_call(
        functools.partial(
            merge_kernel, heads=heads, blocks=blocks, group=group, per=per, scale=scale
        ),
        grid_spec=pltpu.PrefetchScalarGridSpec(
            num_scalar_prefetch=3,
            grid=(blocks // per,),
            in_specs=[
                pl.BlockSpec((heads, per * rows, dh), lambda b, *_: (0, b, 0)),
                pl.BlockSpec((heads, per, rows, dh), lambda b, *_: (0, b, 0, 0)),
                pl.BlockSpec((per, heads, rows), lambda b, *_: (b, 0, 0)),
                pl.BlockSpec(memory_space=pl.ANY),
                pl.BlockSpec(memory_space=pl.ANY),
            ],
            out_specs=pl.BlockSpec((per * BS, q_heads, dh), lambda b, *_: (b, 0, 0)),
            scratch_shapes=[
                pltpu.VMEM((2, per, heads, 2, BS, dh), jnp.bfloat16),
                pltpu.SemaphoreType.DMA((2,)),
            ],
        ),
        out_shape=jax.ShapeDtypeStruct((tok, q_heads, dh), jnp.bfloat16),
        compiler_params=pltpu.CompilerParams(vmem_limit_bytes=56 * 1024 * 1024),
        cost_estimate=pl.CostEstimate(
            flops=4 * heads * blocks * rows * dh * BS,
            bytes_accessed=25_000_000,
            transcendentals=heads * blocks * rows * BS,
        ),
        name="far_merge",
    )(
        owner_at, my_place, valid,
        q_t, local_out, local_lse.transpose(1, 0, 2), first_got, second_got,
    )


def solution(mesh):
    split = P(AXES, None, None)
    return jax.shard_map(
        shards,
        mesh=mesh,
        in_specs=(split, split, split, P(), P(), P()),
        out_specs=split,
        check_vma=False,
    )
```

```python
import functools

import jax
import jax.numpy as jnp
from jax import lax
from jax.experimental import pallas as pl
from jax.experimental.pallas import tpu as pltpu
from jax.sharding import PartitionSpec as P

BS = 64
NW = 8
CAP = 2
AXES = ("blk", "grid")
MASKED = -1e30
LOG2E = 1.4426950408889634


def local_kernel(
    core_sm, slot_sm, off_sm, first_sm,
    q_ref, ko_ref, vo_ref, kh_ref, vh_ref, bias_ref, mine_hbm, other_hbm,
    out_ref, lse_ref,
    kx, vx, kv_buf, vv_buf, lse_buf, sems,
    *, heads, verts, blocks, group, near, scale,
):
    h = pl.program_id(0)
    halo = kh_ref.shape[1]
    own = ko_ref.shape[1]
    dh = q_ref.shape[2]
    left = pl.ds(0, dh)

    def fetch(head, buf):
        def copies(k_from, v_from):
            for i in range(verts):
                slot = slot_sm[head, i]
                rows = pl.ds(i * BS, BS)
                pltpu.make_async_copy(
                    k_from(slot), kv_buf.at[buf, rows], sems.at[buf, 0]
                ).start()
                pltpu.make_async_copy(
                    v_from(slot), vv_buf.at[buf, rows, left], sems.at[buf, 1]
                ).start()

        mine = lambda slot: mine_hbm.at[slot, 2]
        other = lambda slot: other_hbm.at[slot]

        @pl.when(core_sm[0] == 0)
        def _():
            copies(mine, other)

        @pl.when(core_sm[0] != 0)
        def _():
            copies(other, mine)

    @pl.when(h == 0)
    def _():
        vx[:, dh:] = jnp.ones((halo + own, dh), jnp.bfloat16)
        for buf in range(2):
            vv_buf[buf, :, dh:] = jnp.ones((verts * BS, dh), jnp.bfloat16)
        fetch(0, 0)

    @pl.when(h + 1 < heads)
    def _():
        fetch(h + 1, (h + 1) % 2)

    kx[0:halo] = kh_ref[0]
    kx[halo : halo + own] = ko_ref[0]
    vx[0:halo, :dh] = vh_ref[0]
    vx[halo : halo + own, :dh] = vo_ref[0]
    cur = h % 2
    pltpu.make_async_copy(kv_buf.at[cur], kv_buf.at[cur], sems.at[cur, 0]).wait()
    pltpu.make_async_copy(
        vv_buf.at[cur, :, left], vv_buf.at[cur, :, left], sems.at[cur, 1]
    ).wait()

    t_pos = lax.broadcasted_iota(jnp.int32, (group * BS, near * BS), 0) // group
    u_pos = lax.broadcasted_iota(jnp.int32, (group * BS, near * BS), 1)
    causal_bias = jnp.where((u_pos < BS) & (u_pos > t_pos), MASKED, 0.0)
    lane = lax.broadcasted_iota(jnp.int32, (1, near * BS), 1) // BS

    zero_at = jnp.int32(0)
    for i in range(1, near):
        zero_at = jnp.where(off_sm[h, i] == 0, i, zero_at)

    def one_block(b, carry):
        rows = pl.multiple_of(b * group * BS, group * BS)
        q = q_ref[0, pl.ds(rows, group * BS), :]
        k_parts = []
        v_parts = []
        row_bias = jnp.zeros((1, near * BS), jnp.float32)
        for i in range(near):
            off = off_sm[h, lax.rem(zero_at + i, near)]
            start = pl.multiple_of((b + NW - 1 - off) * BS, BS)
            k_parts.append(kx[pl.ds(start, BS), :])
            v_parts.append(vx[pl.ds(start, BS), :])
            miss = jnp.where(first_sm[0] + b < off, MASKED, 0.0)
            row_bias = jnp.where(lane == i, miss, row_bias)
        k_near = jnp.concatenate(k_parts, axis=0)
        v_near = jnp.concatenate(v_parts, axis=0)
        dims = (((1,), (1,)), ((), ()))
        s_near = lax.dot_general(q, k_near, dims, preferred_element_type=jnp.float32)
        s_near = s_near + (causal_bias + row_bias)
        s_vert = lax.dot_general(q, kv_buf[cur], dims, preferred_element_type=jnp.float32)
        s_vert = s_vert + bias_ref[0, pl.ds(b, 1), :]
        top = jnp.maximum(
            jnp.max(s_near, axis=1, keepdims=True), jnp.max(s_vert, axis=1, keepdims=True)
        )
        p_near = jnp.exp2((s_near - top) * (scale * LOG2E)).astype(jnp.bfloat16)
        p_vert = jnp.exp2((s_vert - top) * (scale * LOG2E)).astype(jnp.bfloat16)
        acc = jnp.dot(p_near, v_near, preferred_element_type=jnp.float32)
        acc = acc + jnp.dot(p_vert, vv_buf[cur], preferred_element_type=jnp.float32)
        total = acc[:, dh:]
        out_ref[0, b] = acc[:, :dh] / total
        column = lax.broadcasted_iota(jnp.int32, total.shape, 1) == b
        lse_buf[...] = jnp.where(column, top * scale + jnp.log(total), lse_buf[...])
        return carry

    lax.fori_loop(0, blocks, one_block, 0, unroll=True)
    lse_ref[0] = lse_buf[...].T[:blocks]


def pack_kernel(tile_sm, vert_sm, k_ref, v_ref, out_ref):
    base = pl.program_id(0) * out_ref.shape[0]
    for d in range(out_ref.shape[0]):
        tile = tile_sm[base + d]
        out_ref[d, 0] = k_ref[tile]
        out_ref[d, 1] = v_ref[tile]
        out_ref[d, 2] = (v_ref if d % 2 else k_ref)[vert_sm[0]]


def pack_second_kernel(tile_sm, k_ref, v_ref, out_ref):
    base = pl.program_id(0) * out_ref.shape[0]
    for d in range(out_ref.shape[0]):
        tile = tile_sm[base + d]
        out_ref[d, 0] = k_ref[tile]
        out_ref[d, 1] = v_ref[tile]


def merge_kernel(
    owner_sm, place_sm, valid_sm,
    q_ref, local_ref, lse_ref, first_hbm, second_hbm,
    out_ref,
    kv_buf, sems,
    *, heads, blocks, group, per, scale,
):
    step = pl.program_id(0)

    def fetch(at, buf):
        for j in range(per):
            for h in range(heads):
                request = h * blocks + at * per + j
                owner = owner_sm[request]
                to = kv_buf.at[buf, j, h]

                @pl.when(place_sm[request] == 0)
                def _():
                    pltpu.make_async_copy(
                        first_hbm.at[owner, pl.ds(0, 2)], to, sems.at[buf]
                    ).start()

                @pl.when(place_sm[request] != 0)
                def _():
                    pltpu.make_async_copy(second_hbm.at[owner], to, sems.at[buf]).start()

    @pl.when(step == 0)
    def _():
        fetch(0, 0)

    @pl.when(step + 1 < blocks // per)
    def _():
        fetch(step + 1, (step + 1) % 2)

    cur = step % 2
    pltpu.make_async_copy(kv_buf.at[cur], kv_buf.at[cur], sems.at[cur]).wait()
    rows = group * BS
    dh = q_ref.shape[2]
    head_row = lax.broadcasted_iota(jnp.int32, (heads, 1), 0)
    low = lax.broadcasted_iota(jnp.int32, (rows // 8, 8, dh), 1) < group
    for j in range(per):
        weights = []
        tops = []
        totals = []
        for h in range(heads):
            s = lax.dot_general(
                kv_buf[cur, j, h, 0], q_ref[h, j * rows : (j + 1) * rows, :],
                (((1,), (1,)), ((), ())), preferred_element_type=jnp.float32,
            )
            top = jnp.max(s, axis=0, keepdims=True)
            p = jnp.exp2((s - top) * (scale * LOG2E))
            weights.append(p)
            tops.append(top)
            totals.append(jnp.sum(p, axis=0, keepdims=True))
        total = jnp.concatenate(totals, axis=0)
        far_lse = jnp.concatenate(tops, axis=0) * scale + jnp.log(total)
        local_lse = lse_ref[j]
        joint = jnp.maximum(local_lse, far_lse)
        valid = jnp.zeros((heads, 1), jnp.int32)
        for h in range(heads):
            valid = jnp.where(head_row == h, valid_sm[h * blocks + step * per + j], valid)
        a = jnp.where(valid > 0, jnp.exp(local_lse - joint), 1.0)
        c = jnp.where(valid > 0, jnp.exp(far_lse - joint), 0.0)
        local_share = (a / (a + c)).T
        far_share = c / ((a + c) * total)

        for quad in range(heads // 4):
            wide = []
            for pair in (2 * quad, 2 * quad + 1):
                halves = []
                for h in (2 * pair, 2 * pair + 1):
                    p = (weights[h] * far_share[h : h + 1]).astype(jnp.bfloat16)
                    acc = lax.dot_general(
                        p, kv_buf[cur, j, h, 1], (((0,), (0,)), ((), ())),
                        preferred_element_type=jnp.float32,
                    )
                    mixed = local_share[:, h : h + 1] * local_ref[h, j] + acc
                    halves.append(mixed.reshape(rows // 8, 8, dh))
                x, y = halves
                even = jnp.where(low, x, pltpu.roll(y, group, 1))
                odd = jnp.where(low, pltpu.roll(x, group, 1), y)
                wide.append(jnp.stack([even, odd], axis=1).reshape(BS, 8, dh))
            both = jnp.concatenate(wide, axis=1)
            out_ref[j * BS : (j + 1) * BS, quad * 16 : (quad + 1) * 16, :] = both.astype(
                jnp.bfloat16
            )


def shards(queries, keys, values, vert_blocks, slash_offsets, far_blocks):
    tok, q_heads, dh = queries.shape
    heads = keys.shape[1]
    group = q_heads // heads
    blocks = tok // BS
    verts = vert_blocks.shape[1]
    near = slash_offsets.shape[1]
    reqs = heads * blocks
    devices = lax.axis_size(AXES)
    rank = lax.axis_index(AXES)
    core = rank % 2
    scale = dh**-0.5
    halo_rows = (NW - 1) * BS
    rows = group * BS

    forward = [(i, i + 1) for i in range(devices - 1)]
    rim_k, values = lax.optimization_barrier((keys[tok - halo_rows :], values))
    halo_k = lax.ppermute(rim_k, AXES, forward)
    halo_v = lax.ppermute(values[tok - halo_rows :], AXES, forward)

    k_t = keys.transpose(1, 0, 2)
    v_t = values.transpose(1, 0, 2)

    vert_here = vert_blocks - rank * blocks
    vert_tile = jnp.max(
        jnp.where(
            (vert_here >= 0) & (vert_here < blocks),
            vert_here + jnp.arange(heads)[:, None] * blocks,
            0,
        )
    )

    all_far = far_blocks.reshape(heads, devices, blocks).transpose(1, 0, 2).reshape(devices, reqs)
    earlier = (jnp.arange(reqs)[:, None] < jnp.arange(reqs)[None, :]).astype(jnp.float32)
    asked = (all_far >= 0) & (all_far // blocks == rank)
    place = jnp.dot(asked.astype(jnp.float32), earlier).astype(jnp.int32)
    tile = (jnp.arange(reqs)[None, :] // blocks) * blocks + all_far - rank * blocks
    wanted = asked[:, None, :] & (place[:, None, :] == jnp.arange(CAP)[None, :, None])
    send_tile = jnp.max(jnp.where(wanted, tile[:, None, :], 0), axis=2)
    chunk = 16
    whole = pl.BlockSpec((reqs, BS, dh), lambda i, *_: (0, 0, 0))
    first_send = pl.pallas_call(
        pack_kernel,
        grid_spec=pltpu.PrefetchScalarGridSpec(
            num_scalar_prefetch=2,
            grid=(devices // chunk,),
            in_specs=[whole, whole],
            out_specs=pl.BlockSpec((chunk, 3, BS, dh), lambda i, *_: (i, 0, 0, 0)),
        ),
        out_shape=jax.ShapeDtypeStruct((devices, 3, BS, dh), jnp.bfloat16),
        compiler_params=pltpu.CompilerParams(vmem_limit_bytes=32 * 1024 * 1024),
        name="pack_first",
    )(
        send_tile[:, 0], vert_tile.reshape(1),
        k_t.reshape(reqs, BS, dh), v_t.reshape(reqs, BS, dh),
    )
    first_got = lax.all_to_all(first_send, AXES, split_axis=0, concat_axis=0, tiled=True)
    second, halo_k, halo_v = lax.optimization_barrier((send_tile[:, 1], halo_k, halo_v))
    second_send = pl.pallas_call(
        pack_second_kernel,
        grid_spec=pltpu.PrefetchScalarGridSpec(
            num_scalar_prefetch=1,
            grid=(devices // chunk,),
            in_specs=[whole, whole],
            out_specs=pl.BlockSpec((chunk, 2, BS, dh), lambda i, *_: (i, 0, 0, 0)),
        ),
        out_shape=jax.ShapeDtypeStruct((devices, 2, BS, dh), jnp.bfloat16),
        compiler_params=pltpu.CompilerParams(vmem_limit_bytes=32 * 1024 * 1024),
        cost_estimate=pl.CostEstimate(
            flops=10**12, bytes_accessed=6_000_000, transcendentals=0
        ),
        name="pack_second",
    )(second, k_t.reshape(reqs, BS, dh), v_t.reshape(reqs, BS, dh))
    my_far = lax.dynamic_slice_in_dim(far_blocks, rank * blocks, blocks, 1).reshape(-1)
    valid = (my_far >= 0).astype(jnp.int32)
    owner = jnp.where(my_far >= 0, my_far // blocks, -1)
    same = owner[:, None] == owner[None, :]
    my_place = jnp.sum(same & (jnp.arange(reqs)[None, :] < jnp.arange(reqs)[:, None]), axis=1)

    q_t = queries.reshape(tok, heads, group, dh).transpose(1, 0, 2, 3).reshape(heads, tok * group, dh)
    my_blocks = rank * blocks + jnp.arange(blocks)
    vert_ok = vert_blocks[:, None, :] <= my_blocks[None, :, None] - NW
    vert_bias = jnp.repeat(jnp.where(vert_ok, 0.0, MASKED).astype(jnp.float32), BS, axis=2)

    owner_at = jnp.maximum(owner, 0).astype(jnp.int32)
    my_place = my_place.astype(jnp.int32)
    second_send, first_got, halo_k, halo_v, q_t, vert_bias, owner_at, my_place, valid = (
        lax.optimization_barrier(
            (
                second_send, first_got, halo_k, halo_v,
                q_t, vert_bias, owner_at, my_place, valid,
            )
        )
    )
    vert_other = lax.ppermute(first_got[:, 2], AXES, [(i, i ^ 1) for i in range(devices)])
    second_got = lax.all_to_all(second_send, AXES, split_axis=0, concat_axis=0, tiled=True)

    by_head = lambda *tail: pl.BlockSpec((1,) + tail, lambda h, *_: (h,) + (0,) * len(tail))
    local_out, local_lse = pl.pallas_call(
        functools.partial(
            local_kernel, heads=heads, verts=verts, blocks=blocks, group=group, near=near,
            scale=scale,
        ),
        grid_spec=pltpu.PrefetchScalarGridSpec(
            num_scalar_prefetch=4,
            grid=(heads,),
            in_specs=[
                by_head(tok * group, dh),
                by_head(tok, dh),
                by_head(tok, dh),
                by_head(halo_rows, dh),
                by_head(halo_rows, dh),
                by_head(blocks, verts * BS),
                pl.BlockSpec(memory_space=pltpu.HBM),
                pl.BlockSpec(memory_space=pltpu.HBM),
            ],
            out_specs=[by_head(blocks, rows, dh), by_head(blocks, rows)],
            scratch_shapes=[
                pltpu.VMEM((halo_rows + tok, dh), jnp.bfloat16),
                pltpu.VMEM((halo_rows + tok, 2 * dh), jnp.bfloat16),
                pltpu.VMEM((2, verts * BS, dh), jnp.bfloat16),
                pltpu.VMEM((2, verts * BS, 2 * dh), jnp.bfloat16),
                pltpu.VMEM((rows, 128), jnp.float32),
                pltpu.SemaphoreType.DMA((2, 2)),
            ],
        ),
        out_shape=[
            jax.ShapeDtypeStruct((heads, blocks, rows, dh), jnp.float32),
            jax.ShapeDtypeStruct((heads, blocks, rows), jnp.float32),
        ],
        compiler_params=pltpu.CompilerParams(vmem_limit_bytes=56 * 1024 * 1024),
        cost_estimate=pl.CostEstimate(
            flops=400 * heads * blocks * rows * dh * (near + verts) * BS,
            bytes_accessed=40_000_000,
            transcendentals=heads * blocks * rows * (near + verts) * BS,
        ),
        name="local_attention",
    )(
        core.reshape(1).astype(jnp.int32),
        (vert_blocks // blocks).astype(jnp.int32),
        slash_offsets,
        (rank * blocks).reshape(1).astype(jnp.int32),
        q_t, k_t, v_t, halo_k.transpose(1, 0, 2), halo_v.transpose(1, 0, 2), vert_bias, first_got, vert_other,
    )

    per = 2 if blocks % 2 == 0 else 1
    return pl.pallas_call(
        functools.partial(
            merge_kernel, heads=heads, blocks=blocks, group=group, per=per, scale=scale
        ),
        grid_spec=pltpu.PrefetchScalarGridSpec(
            num_scalar_prefetch=3,
            grid=(blocks // per,),
            in_specs=[
                pl.BlockSpec((heads, per * rows, dh), lambda b, *_: (0, b, 0)),
                pl.BlockSpec((heads, per, rows, dh), lambda b, *_: (0, b, 0, 0)),
                pl.BlockSpec((per, heads, rows), lambda b, *_: (b, 0, 0)),
                pl.BlockSpec(memory_space=pl.ANY),
                pl.BlockSpec(memory_space=pl.ANY),
            ],
            out_specs=pl.BlockSpec((per * BS, q_heads, dh), lambda b, *_: (b, 0, 0)),
            scratch_shapes=[
                pltpu.VMEM((2, per, heads, 2, BS, dh), jnp.bfloat16),
                pltpu.SemaphoreType.DMA((2,)),
            ],
        ),
        out_shape=jax.ShapeDtypeStruct((tok, q_heads, dh), jnp.bfloat16),
        compiler_params=pltpu.CompilerParams(vmem_limit_bytes=56 * 1024 * 1024),
        cost_estimate=pl.CostEstimate(
            flops=4 * heads * blocks * rows * dh * BS,
            bytes_accessed=25_000_000,
            transcendentals=heads * blocks * rows * BS,
        ),
        name="far_merge",
    )(
        owner_at, my_place, valid,
        q_t, local_out, local_lse.transpose(1, 0, 2), first_got, second_got,
    )


def solution(mesh):
    split = P(AXES, None, None)
    return jax.shard_map(
        shards,
        mesh=mesh,
        in_specs=(split, split, split, P(), P(), P()),
        out_specs=split,
        check_vma=False,
    )
```
